256 devices in a mesh: ctx: 32 (over y_lo, z, core), fsdp: 8 (over x, y_hi).
Axes of the slice: x: 4, y: 4 (y_hi: 2, y_lo: 2; y = y_hi * 2 + y_lo), z: 8, core: 2. Of those that a mesh axis runs over, the one named last changes fastest.
Arguments:
- queries: bfloat16 [8, 4096, 2048], P('fsdp', 'ctx'), may hold values from -8 to 8
- keys_values: bfloat16 [8, 4096, 2, 2048], P('fsdp', 'ctx'), may hold values from -8 to 8
- upstream: bfloat16 [8, 4096, 2048], P('fsdp', 'ctx'), may hold values from -6 to 6
- out_weight: bfloat16 [2048, 2048], P('fsdp'), may hold values from -0.125 to 0.125
Outputs:
- grad_queries: bfloat16 [8, 4096, 2048], P('fsdp', 'ctx')
- grad_keys_values: bfloat16 [8, 4096, 2, 2048], P('fsdp', 'ctx')
- grad_weight: float32 [2048, 2048], P(('ctx', 'fsdp'))
The draws below stay inside these ranges and needn't reach their ends.
All inputs are finite; a program needn't handle non-finite values.
Results may differ from the reference program's by a relative error of at most 0.014.
Values may be sent and summed in bfloat16 or wider, within the bound.
No kernel may reach another device: no remote copies, remote signals or barrier semaphores. Data moves between devices by JAX's collectives and lax.ppermute only.
A program may use at most 128 MiB of HBM per device.

```python
import jax
import jax.numpy as jnp
from jax import lax

D = 2048
HEADS = 16
HEAD_DIM = 128
ATTN = 2048
TOK_DEV = 128
SPAN = 4
WINDOW = 512
SEQ_DEV = 1
SEQ = 4096
SEQS = 8
N_CTX = 32
N_FSDP = 8


def draw_queries(key, part):
    result = jnp.clip(jax.random.normal(jax.random.fold_in(key, 11), (SEQS, SEQ, ATTN), jnp.float32), -4.0, 4.0)
    return result.astype(jnp.bfloat16)


def draw_keys_values(key, part):
    key_part = jnp.clip(jax.random.normal(jax.random.fold_in(key, 21), (SEQS, SEQ, ATTN), jnp.float32), -4.0, 4.0)
    value_part = jnp.clip(jax.random.normal(jax.random.fold_in(key, 23), (SEQS, SEQ, ATTN), jnp.float32), -4.0, 4.0)
    return jnp.stack([key_part, value_part], axis=2).astype(jnp.bfloat16)


def spiked(values, own_key, source, target, parts, factor):
    def block_of(axis_at):
        return (jnp.arange(values.shape[axis_at]) // (values.shape[axis_at] // parts)).reshape((-1,) + (1,) * (values.ndim - 1 - axis_at))

    near = jax.random.permutation(own_key, parts)[block_of(target)]
    other_side = (block_of(target) + parts // 2) % parts
    return jnp.where((block_of(source) == near) | (block_of(source) == other_side), factor * values, values)


def levels(stream_key, dims, cuts, smallest, top_value):
    level, own = 1.0, jax.random.fold_in(stream_key, 6)
    for axis_at, parts in cuts:
        steps = jnp.exp(jax.random.uniform(jax.random.fold_in(own, axis_at), (parts,), jnp.float32, smallest / len(cuts), top_value / len(cuts)))
        level = level * jnp.repeat(steps, dims[axis_at] // parts).reshape([-1 if axis == axis_at else 1 for axis in range(len(dims))])
    return level


def scatter_about(rng, shape, width, reach, split=(), kind=jnp.bfloat16):
    drawn = jax.random.normal(rng, shape, jnp.float32) * width
    if len(split) > 0:
        drawn = levels(rng, shape, split, -0.22, 0.18) * drawn
    return jnp.clip(drawn, min=-reach, max=reach).astype(kind)


def gaussian_with(own_key, dims, width, bound, cuts, heavy, kind=jnp.bfloat16):
    values = width * jax.random.normal(own_key, dims, jnp.float32)
    if cuts:
        values = values * levels(own_key, dims, cuts, -0.22, 0.18)
    return jnp.clip(spiked(values, jax.random.fold_in(own_key, 3), *heavy), -bound, bound).astype(kind)


def setup_inputs(seed: int = 0) -> dict:
    key_of = jax.random.split(jax.random.key(seed), 5)
    queries = draw_queries(jax.random.fold_in(key_of[4], 71), 0)
    keys_values = draw_keys_values(jax.random.fold_in(key_of[4], 71), 0)
    upstream = gaussian_with(key_of[2], (SEQS, SEQ, D), 1.0, 6.0, ((0, 8), (1, 32)), (1, 2, 32, 2.75))
    out_weight = scatter_about(key_of[3], (D, ATTN), ATTN ** -0.5, 0.125, ((0, 8),))
    return {"queries": queries, "keys_values": keys_values, "upstream": upstream, "out_weight": out_weight}


NEGATIVE = -1e30


def one_sequence(inputs):
    query_seq, pair_seq, grad_seq = inputs
    padding = SPAN * TOK_DEV
    key_count = (SPAN + 1) * TOK_DEV
    inv_root = HEAD_DIM ** -0.5
    padded_pairs = jnp.concatenate([jnp.zeros((padding, 2, ATTN), jnp.bfloat16), pair_seq], axis=0)

    def block_step(carried, block_index):
        first_row = (block_index * TOK_DEV).astype(jnp.int32)
        query_block = lax.dynamic_slice_in_dim(query_seq, first_row, TOK_DEV, 0).astype(jnp.float32).reshape(TOK_DEV, HEADS, HEAD_DIM)
        grad_block = lax.dynamic_slice_in_dim(grad_seq, first_row, TOK_DEV, 0).reshape(TOK_DEV, HEADS, HEAD_DIM)
        pair_window = lax.dynamic_slice_in_dim(padded_pairs, first_row, key_count, 0)
        key_heads = pair_window[:, 0].astype(jnp.float32).reshape(key_count, HEADS, HEAD_DIM)
        value_heads = pair_window[:, 1].astype(jnp.float32).reshape(key_count, HEADS, HEAD_DIM)
        query_pos = first_row + jnp.arange(TOK_DEV, dtype=jnp.int32)
        key_pos = first_row - padding + jnp.arange(key_count, dtype=jnp.int32)
        distance = query_pos[:, None] - key_pos[None, :]
        visible = (distance >= 0) & (distance < WINDOW) & (key_pos[None, :] >= 0)
        scores = jnp.einsum('qhe,khe->hqk', query_block, key_heads) * inv_root
        scores = jnp.where(visible[None], scores, NEGATIVE)
        row_max = jnp.max(scores, axis=-1, keepdims=True)
        lifted = jnp.exp(scores - row_max)
        probability = lifted / jnp.sum(lifted, axis=-1, keepdims=True)
        probs_low = probability.astype(jnp.bfloat16)
        attended = jnp.einsum('hqk,khe->qhe', probs_low.astype(jnp.float32), value_heads).astype(jnp.bfloat16)
        grad_f = grad_block.astype(jnp.float32)
        products = jnp.einsum('qhe,khe->hqk', grad_f, value_heads)
        center = jnp.sum(grad_f * attended.astype(jnp.float32), axis=-1)
        center = jnp.swapaxes(center, 0, 1)[:, :, None]
        grad_scores = (probability * (products - center)).astype(jnp.bfloat16).astype(jnp.float32)
        grad_queries = (jnp.einsum('hqk,khe->qhe', grad_scores, key_heads) * inv_root).astype(jnp.bfloat16)
        grad_keys = jnp.einsum('hqk,qhe->khe', grad_scores, query_block) * inv_root
        grad_values = jnp.einsum('hqk,qhe->khe', probs_low.astype(jnp.float32), grad_f)
        grad_window = jnp.stack([grad_keys.reshape(key_count, ATTN), grad_values.reshape(key_count, ATTN)], axis=1)
        previous = lax.dynamic_slice_in_dim(carried, first_row, key_count, 0)
        carried = lax.dynamic_update_slice_in_dim(carried, previous + grad_window, first_row, 0)
        return carried, (attended.reshape(TOK_DEV, ATTN), grad_queries.reshape(TOK_DEV, ATTN))

    start_carry = jnp.zeros((SEQ + padding, 2, ATTN), jnp.float32)
    carried, outputs = lax.scan(block_step, start_carry, jnp.arange(N_CTX, dtype=jnp.int32))
    attended_all = outputs[0].reshape(SEQ, ATTN)
    grad_query_all = outputs[1].reshape(SEQ, ATTN)
    return attended_all, grad_query_all, carried[padding:].astype(jnp.bfloat16)


def reference(queries, keys_values, upstream, out_weight):
    grad_attended = jnp.dot(upstream.reshape(SEQS * SEQ, D), out_weight, preferred_element_type=jnp.float32)
    grad_attended = grad_attended.astype(jnp.bfloat16).reshape(SEQS, SEQ, ATTN)
    attended, grad_queries, grad_keys_values = lax.map(one_sequence, (queries, keys_values, grad_attended))
    attended_dev = attended.reshape(N_FSDP, SEQ_DEV, N_CTX, TOK_DEV, ATTN).transpose(0, 2, 1, 3, 4)
    attended_dev = attended_dev.reshape(N_FSDP * N_CTX, SEQ_DEV * TOK_DEV, ATTN)
    upstream_dev = upstream.reshape(N_FSDP, SEQ_DEV, N_CTX, TOK_DEV, D).transpose(0, 2, 1, 3, 4)
    upstream_dev = upstream_dev.reshape(N_FSDP * N_CTX, SEQ_DEV * TOK_DEV, D)

    def add_partial(running, pieces):
        weight_term = lax.dot_general(pieces[0], pieces[1], (((0,), (0,)), ((), ())), preferred_element_type=jnp.float32)
        weight_term = lax.optimization_barrier(weight_term.astype(jnp.bfloat16)).astype(jnp.float32)
        return running + weight_term, None

    grad_weight, unused_out = lax.scan(add_partial, jnp.zeros((D, ATTN), jnp.float32), (upstream_dev, attended_dev))
    return grad_queries, grad_keys_values, grad_weight
```

```python
import functools

import jax
import jax.numpy as jnp
from jax import lax
from jax.experimental import pallas as pl
from jax.experimental.pallas import tpu as pltpu
from jax.sharding import Mesh
from jax.sharding import PartitionSpec as P

SPLIT = (("yl", 2), ("z", 8), ("core", 2), ("x", 4), ("yh", 2))
CTX = ("yl", "z", "core")
FSDP = ("x", "yh")

TOK = 128
CHIP = 256
HEADS = 8
HD = 128
HALF = HEADS * HD
D = 2048
NEGATIVE = -1e30
INV_ROOT = HD**-0.5
BF = jnp.bfloat16
F32 = jnp.float32


def dot(a, b, ca, cb):
    return lax.dot_general(a, b, (((ca,), (cb,)), ((), ())), preferred_element_type=F32)


def to_chip(a, by, cross):
    pairs = []
    for i in range(16):
        for core in range(2):
            if 0 <= i + by < 16:
                pairs.append((2 * i + core, 2 * (i + by) + (1 - core if cross else core)))
    return lax.ppermute(a, CTX, pairs)


def to_core(a):
    return lax.ppermute(a, "core", [(0, 1), (1, 0)])


def to_x(a, by):
    return lax.ppermute(a, "x", [(i, (i + by) % 4) for i in range(4)])


def to_y_neighbour(a):
    return lax.ppermute(a, ("yl", "yh"), [(0, 3), (3, 0), (1, 2), (2, 1)])


def project_kernel(s_ref, up_own, up_oth, w0, w1, w3, wa, wb, out):
    x, yh = s_ref[2], s_ref[3]
    total = None
    pieces = [(0, 0, w0, 0), (0, 1, w0, 256), (1, 0, w1, 0), (1, 1, w1, 256)]
    pieces += [(3, 0, w3, 0), (3, 1, w3, 256), (2, 0, wa, 0), (2, 1, wb, 0)]
    for dx, dy, ref, start in pieces:
        block = ((x + dx) & 3) * 2 + ((yh + dy) & 1)
        at = pl.ds(pl.multiple_of(block * 256, 256), 256)
        left = jnp.concatenate([up_own[:, at], up_oth[:, at]], axis=0)
        part = dot(left, ref[start : start + 256, :], 1, 0)
        total = part if total is None else total + part
    out[...] = total.astype(BF)


def project(scalars, up_own, up_oth, w0, w1, w3, wa, wb):
    width = w0.shape[1]
    tile = 256
    whole = lambda rows: pl.BlockSpec((rows, D), lambda n, s: (0, 0))
    cols = lambda rows: pl.BlockSpec((rows, tile), lambda n, s: (0, n))
    return pl.pallas_call(
        project_kernel,
        grid_spec=pltpu.PrefetchScalarGridSpec(
            num_scalar_prefetch=1,
            grid=(width // tile,),
            in_specs=[whole(TOK), whole(TOK), cols(512), cols(512), cols(512), cols(256), cols(256)],
            out_specs=cols(CHIP),
        ),
        out_shape=jax.ShapeDtypeStruct((CHIP, width), BF),
        compiler_params=pltpu.CompilerParams(vmem_limit_bytes=32 << 20),
        cost_estimate=pl.CostEstimate(
            flops=2 * CHIP * D * width, bytes_accessed=2 * D * width + 3 * CHIP * D, transcendentals=0
        ),
        name="project",
    )(scalars, up_own, up_oth, w0, w1, w3, wa, wb)


def attention_kernel(
    s_ref, q_own, q_oth, k_own, k_oth, v_own, v_oth, k1r, v1r, k2r, v2r, do_r,
    att_r, own_r, oth_r, g1_r, g2_r,
):
    core, chip = s_ref[0], s_ref[1]
    q = jnp.concatenate([q_own[...], q_oth[...]], axis=0)
    k0 = jnp.concatenate([k_own[...], k_oth[...]], axis=0)
    v0 = jnp.concatenate([v_own[...], v_oth[...]], axis=0)
    k1, v1, k2, v2 = k1r[...], v1r[...], k2r[...], v2r[...]
    do = do_r[...]
    key_at = (lax.broadcasted_iota(jnp.int32, (CHIP, CHIP), 0) + core * TOK) & (CHIP - 1)
    query_at = (lax.broadcasted_iota(jnp.int32, (CHIP, CHIP), 1) + core * TOK) & (CHIP - 1)
    near = key_at <= query_at
    shown = jnp.logical_or(near, chip >= 2)
    sm = jnp.where(near, dot(k0, q, 1, 1), dot(k2, q, 1, 1)) * INV_ROOT
    sm = jnp.where(shown, sm, NEGATIVE)
    s1 = jnp.where(chip >= 1, dot(k1, q, 1, 1) * INV_ROOT, NEGATIVE)
    top = jnp.maximum(jnp.max(sm, axis=0, keepdims=True), jnp.max(s1, axis=0, keepdims=True))
    em = jnp.exp(sm - top)
    e1 = jnp.exp(s1 - top)
    scale = 1.0 / (jnp.sum(em, axis=0, keepdims=True) + jnp.sum(e1, axis=0, keepdims=True))
    pm = em * scale
    p1 = e1 * scale
    p1_low = p1.astype(BF)
    p0_low = jnp.where(near, pm, 0.0).astype(BF)
    p2_low = jnp.where(near, 0.0, pm).astype(BF)
    att_t = dot(v0.T, p0_low, 1, 0) + dot(v1.T, p1_low, 1, 0) + dot(v2.T, p2_low, 1, 0)
    att_t = att_t.astype(BF)
    att_r[...] = att_t.T
    center = jnp.sum(do.T.astype(F32) * att_t.astype(F32), axis=0, keepdims=True)
    dm = pm * (jnp.where(near, dot(v0, do, 1, 1), dot(v2, do, 1, 1)) - center)
    d1 = (p1 * (dot(v1, do, 1, 1) - center)).astype(BF)
    d0 = jnp.where(near, dm, 0.0).astype(BF)
    d2 = jnp.where(near, 0.0, dm).astype(BF)
    dq_t = dot(k0.T, d0, 1, 0) + dot(k1.T, d1, 1, 0) + dot(k2.T, d2, 1, 0)
    dq = (dq_t * INV_ROOT).astype(BF).T
    g1_r[0] = (dot(d1, q, 1, 0) * INV_ROOT).astype(BF)
    g1_r[1] = dot(p1_low, do, 1, 0).astype(BF)
    g2_r[0] = (dot(d2, q, 1, 0) * INV_ROOT).astype(BF)
    g2_r[1] = dot(p2_low, do, 1, 0).astype(BF)
    dk = (dot(d0, q, 1, 0) * INV_ROOT).astype(BF)
    dv = dot(p0_low, do, 1, 0).astype(BF)
    own_r[0], oth_r[0] = dq[:TOK], dq[TOK:]
    own_r[1], oth_r[1] = dk[:TOK], dk[TOK:]
    own_r[2], oth_r[2] = dv[:TOK], dv[TOK:]


def attention(scalars, queries, swapped, kv_own, kv1, kv2, do):
    at = lambda rows, first: pl.BlockSpec((rows, HD), lambda h, s: (0, first + h))
    deep = lambda n, rows: pl.BlockSpec((n, rows, HD), lambda h, s: (0, 0, h))
    return pl.pallas_call(
        attention_kernel,
        grid_spec=pltpu.PrefetchScalarGridSpec(
            num_scalar_prefetch=1,
            grid=(HEADS,),
            in_specs=[
                pl.BlockSpec((TOK, HD), lambda h, s: (0, s[0] * HEADS + h)),
                at(TOK, 0),
                at(TOK, 0),
                at(TOK, HEADS),
                at(TOK, HEADS),
                at(TOK, 2 * HEADS),
                at(CHIP, 0),
                at(CHIP, HEADS),
                at(CHIP, 0),
                at(CHIP, HEADS),
                at(CHIP, 0),
            ],
            out_specs=[at(CHIP, 0), deep(3, TOK), deep(3, TOK), deep(2, CHIP), deep(2, CHIP)],
        ),
        out_shape=[
            jax.ShapeDtypeStruct((CHIP, HALF), BF),
            jax.ShapeDtypeStruct((3, TOK, HALF), BF),
            jax.ShapeDtypeStruct((3, TOK, HALF), BF),
            jax.ShapeDtypeStruct((2, CHIP, HALF), BF),
            jax.ShapeDtypeStruct((2, CHIP, HALF), BF),
        ],
        compiler_params=pltpu.CompilerParams(vmem_limit_bytes=40 << 20),
        cost_estimate=pl.CostEstimate(
            flops=2 * 18 * CHIP * CHIP * HD * HEADS,
            bytes_accessed=12 << 20,
            transcendentals=2 * CHIP * CHIP * HEADS,
        ),
        name="attention",
    )(scalars, queries, swapped, kv_own, swapped, kv_own, swapped, kv1, kv1, kv2, kv2, do)


def weight_kernel(s_ref, up_t, att, out):
    x = s_ref[2]
    right = att[...]
    for g in range(D // 256):
        part = dot(up_t[256 * g : 256 * (g + 1), :], right, 1, 0)
        part = part.reshape(4, 4, 2, 8, right.shape[1])
        for to in range(4):
            for half in range(2):
                rows = part[:, to, half].reshape(32, right.shape[1])
                out[(to - x) & 3, half, 32 * g : 32 * (g + 1), :] = rows.astype(BF)


def weight_partial(scalars, up_t, att):
    width = att.shape[1]
    tile = 256
    return pl.pallas_call(
        weight_kernel,
        grid_spec=pltpu.PrefetchScalarGridSpec(
            num_scalar_prefetch=1,
            grid=(width // tile,),
            in_specs=[
                pl.BlockSpec((D, CHIP), lambda n, s: (0, 0)),
                pl.BlockSpec((CHIP, tile), lambda n, s: (0, n)),
            ],
            out_specs=pl.BlockSpec((4, 2, 256, tile), lambda n, s: (0, 0, 0, n)),
        ),
        out_shape=jax.ShapeDtypeStruct((4, 2, 256, width), BF),
        compiler_params=pltpu.CompilerParams(vmem_limit_bytes=32 << 20),
        cost_estimate=pl.CostEstimate(
            flops=2 * CHIP * D * width, bytes_accessed=2 * D * width + 3 * CHIP * D, transcendentals=0
        ),
        name="weight_partial",
    )(scalars, up_t, att)


def plus(*terms):
    total = terms[0].astype(F32)
    for t in terms[1:]:
        total = total + t.astype(F32)
    return total


def spread_weight(part):
    width = part.shape[-1]
    a1 = to_x(part[2, 0], 1)
    b1 = to_x(part[2, 1], -1)
    a2 = to_x(jnp.stack([plus(part[1, 0], a1).astype(BF), part[1, 1]]), 1)
    b2 = to_x(jnp.stack([part[3, 0], plus(part[3, 1], b1).astype(BF)]), -1)
    mine = plus(part[0], a2, b2).astype(BF).reshape(4, 128, width)
    mine = lax.all_to_all(mine, ("yh", "yl"), 0, 0, tiled=True)
    mine = jnp.sum(mine.astype(F32), axis=0).astype(BF).reshape(16, 8, width)
    mine = lax.all_to_all(mine, ("z", "core"), 0, 0, tiled=True)
    mine = jnp.sum(mine.reshape(8, 2, 8, width).astype(F32), axis=0)
    return jnp.concatenate([mine[0], mine[1]], axis=1)


def shards(queries, keys_values, upstream, out_weight):
    core = lax.axis_index("core")
    x, yh = lax.axis_index("x"), lax.axis_index("yh")
    chip = lax.axis_index("yl") * 8 + lax.axis_index("z")
    scalars = jnp.stack([core, chip, x, yh]).astype(jnp.int32)
    own, oth = core * HALF, (1 - core) * HALF
    q, up = queries[0], upstream[0]
    kv = keys_values[0].reshape(TOK, 2 * D)
    cut = lambda a, first: lax.dynamic_slice_in_dim(a, first, HALF, 1)
    kv_own = jnp.concatenate([cut(kv, own), cut(kv, D + own)], axis=1)
    kv_oth = jnp.concatenate([cut(kv, oth), cut(kv, D + oth)], axis=1)

    kv1 = jnp.concatenate([to_chip(kv_own, 1, False), to_chip(kv_oth, 1, True)], axis=0)
    swapped = to_core(jnp.concatenate([cut(q, oth), kv_oth, up], axis=1))
    w_own = cut(out_weight, own)
    w0 = jnp.concatenate([w_own, to_y_neighbour(w_own)], axis=0)
    w3 = to_x(w0, 1)
    w1 = to_x(w0, -1)
    wa = to_x(w3[:256], 1)
    wb = to_x(w1[256:], -1)
    kv2 = to_chip(kv1, 1, False)

    up_oth = swapped[:, 3 * HALF :]
    do = project(scalars, up, up_oth, w0, w1, w3, wa, wb)
    att, mine, theirs, g1, g2 = attention(scalars, q, swapped, kv_own, kv1, kv2, do)

    back = to_chip(g2, -1, False)
    got = to_core(theirs)
    up_t = jnp.concatenate([up, up_oth], axis=0).T
    grad_weight = spread_weight(weight_partial(scalars, up_t, att))
    back = plus(g1, back).astype(BF)
    same = to_chip(back[:, :TOK], -1, False)
    cross = to_chip(back[:, TOK:], -1, True)

    def sides(a, b):
        return jnp.where(core == 0, jnp.concatenate([a, b], -1), jnp.concatenate([b, a], -1))

    grad_q = sides(mine[0], got[0])
    grad_kv = sides(plus(mine[1:], same), plus(got[1:], cross)).astype(BF)
    return grad_q[None], jnp.swapaxes(grad_kv, 0, 1)[None], grad_weight


def solution(mesh):
    names = tuple(name for name, _ in SPLIT)
    fine = Mesh(mesh.devices.reshape([size for _, size in SPLIT]), names)
    return jax.shard_map(
        shards,
        mesh=fine,
        in_specs=(P(FSDP, CTX, None), P(FSDP, CTX, None, None), P(FSDP, CTX, None), P(FSDP, None)),
        out_specs=(P(FSDP, CTX, None), P(FSDP, CTX, None, None), P(CTX + FSDP, None)),
        check_vma=False,
    )
```

```python
import jax
import jax.numpy as jnp
from jax import lax
from jax.experimental import pallas as pl
from jax.experimental.pallas import tpu as pltpu
from jax.sharding import Mesh
from jax.sharding import PartitionSpec as P

SPLIT = (("yl", 2), ("z", 8), ("core", 2), ("x", 4), ("yh", 2))
CTX = ("yl", "z", "core")
FSDP = ("x", "yh")

TOK = 128
CHIP = 256
HEADS = 8
HD = 128
HALF = HEADS * HD
D = 2048
CHUNKS = 2
PART = HEADS // CHUNKS
WIDE = PART * HD
NEGATIVE = -1e30
INV_ROOT = HD**-0.5
BF = jnp.bfloat16
F32 = jnp.float32
VMEM = 56 << 20


def dot(a, b, ca, cb):
    return lax.dot_general(a, b, (((ca,), (cb,)), ((), ())), preferred_element_type=F32)


def to_chip(a, by, cross):
    pairs = []
    for i in range(16):
        for core in range(2):
            if 0 <= i + by < 16:
                pairs.append((2 * i + core, 2 * (i + by) + (1 - core if cross else core)))
    return lax.ppermute(a, CTX, pairs)


def to_core(a):
    return lax.ppermute(a, "core", [(0, 1), (1, 0)])


def call(body, name, grid, in_specs, out_specs, out_shape, flops, moved, exps=0):
    return pl.pallas_call(
        body,
        grid_spec=pltpu.PrefetchScalarGridSpec(
            num_scalar_prefetch=1, grid=grid, in_specs=in_specs, out_specs=out_specs
        ),
        out_shape=out_shape,
        compiler_params=pltpu.CompilerParams(vmem_limit_bytes=VMEM),
        cost_estimate=pl.CostEstimate(flops=flops, bytes_accessed=moved, transcendentals=exps),
        name=name,
    )


def whole(*shape):
    return pl.BlockSpec(shape, lambda *_: (0,) * len(shape))


def bf(*shape):
    return jax.ShapeDtypeStruct(shape, BF)


def pairs_kernel(s_ref, kv, *outs):
    own = s_ref[0] * HALF
    for i in range(CHUNKS):
        for side, first in ((0, own), (1, HALF - own)):
            at = pl.ds(pl.multiple_of(first + i * WIDE, HD), WIDE)
            for which in range(2):
                outs[2 * i + side][:, which * WIDE : (which + 1) * WIDE] = kv[which, :, at]


def cut_pairs(scalars, kv):
    return call(
        pairs_kernel, "cut_pairs", (1,), [whole(2, TOK, D)], [whole(TOK, 2 * WIDE)] * (2 * CHUNKS),
        [bf(TOK, 2 * WIDE)] * (2 * CHUNKS), 0, 4 << 20,
    )(scalars, kv)


def swap_kernel(s_ref, up, q, kv, out):
    oth = pl.ds(pl.multiple_of(HALF - s_ref[0] * HALF, HD), HALF)
    out[:, :D] = up[...]
    out[:, D : D + HALF] = q[:, oth]
    out[:, D + HALF : D + 2 * HALF] = kv[0, :, oth]
    out[:, D + 2 * HALF :] = kv[1, :, oth]


def cut_swap(scalars, up, q, kv):
    return call(
        swap_kernel, "cut_swap", (1,), [whole(TOK, D), whole(TOK, D), whole(2, TOK, D)],
        whole(TOK, 5 * HALF), bf(TOK, 5 * HALF), 0, 4 << 20,
    )(scalars, up, q, kv)


def join_kernel(s_ref, up_own, up_oth, up, up_t):
    both = jnp.concatenate([up_own[...], up_oth[...]], axis=0)
    up[...] = both
    turned = both.T.reshape(32, 4, 16, CHIP)
    for to in range(4):
        up_t[to] = turned[:, to].reshape(512, CHIP)


def join(scalars, up_own, swapped):
    return call(
        join_kernel, "join", (1,), [whole(TOK, D), pl.BlockSpec((TOK, D), lambda *_: (0, 0))],
        [whole(CHIP, D), whole(4, 512, CHIP)], [bf(CHIP, D), bf(4, 512, CHIP)], 0, 3 << 20,
    )(scalars, up_own, swapped)


def project_kernel(s_ref, up, w, out):
    out[...] = dot(up[...], w[...], 1, 0).astype(BF)


def project(scalars, up, w):
    tile = 256
    return call(
        project_kernel, "project", (WIDE // tile,),
        [whole(CHIP, D), pl.BlockSpec((D, tile), lambda n, s: (0, n))],
        pl.BlockSpec((CHIP, tile), lambda n, s: (0, n)), bf(CHIP, WIDE),
        2 * CHIP * D * WIDE, 2 * D * WIDE + 3 * CHIP * D,
    )(scalars, up, w)


def attention_kernel(
    s_ref, q_own, q_oth, k_own, k_oth, v_own, v_oth, k1r, v1r, k2r, v2r, do_r,
    att_r, own_r, oth_r, g1_r, g2_r,
):
    core, chip = s_ref[0], s_ref[1]
    q = jnp.concatenate([q_own[...], q_oth[...]], axis=0)
    k0 = jnp.concatenate([k_own[...], k_oth[...]], axis=0)
    v0 = jnp.concatenate([v_own[...], v_oth[...]], axis=0)
    k1, v1, k2, v2 = k1r[...], v1r[...], k2r[...], v2r[...]
    do = do_r[...]
    key_at = (lax.broadcasted_iota(jnp.int32, (CHIP, CHIP), 0) + core * TOK) & (CHIP - 1)
    query_at = (lax.broadcasted_iota(jnp.int32, (CHIP, CHIP), 1) + core * TOK) & (CHIP - 1)
    near = key_at <= query_at
    shown = jnp.logical_or(near, chip >= 2)
    sm = jnp.where(near, dot(k0, q, 1, 1), dot(k2, q, 1, 1)) * INV_ROOT
    sm = jnp.where(shown, sm, NEGATIVE)
    s1 = jnp.where(chip >= 1, dot(k1, q, 1, 1) * INV_ROOT, NEGATIVE)
    top = jnp.maximum(jnp.max(sm, axis=0, keepdims=True), jnp.max(s1, axis=0, keepdims=True))
    em = jnp.exp(sm - top)
    e1 = jnp.exp(s1 - top)
    scale = 1.0 / (jnp.sum(em, axis=0, keepdims=True) + jnp.sum(e1, axis=0, keepdims=True))
    pm = em * scale
    p1 = e1 * scale
    p1_low = p1.astype(BF)
    p0_low = jnp.where(near, pm, 0.0).astype(BF)
    p2_low = jnp.where(near, 0.0, pm).astype(BF)
    att_t = dot(v0.T, p0_low, 1, 0) + dot(v1.T, p1_low, 1, 0) + dot(v2.T, p2_low, 1, 0)
    att_t = att_t.astype(BF)
    att = att_t.T
    for to in range(4):
        att_r[to] = att
    center = jnp.sum(do.T.astype(F32) * att_t.astype(F32), axis=0, keepdims=True)
    dm = pm * (jnp.where(near, dot(v0, do, 1, 1), dot(v2, do, 1, 1)) - center)
    d1 = (p1 * (dot(v1, do, 1, 1) - center)).astype(BF)
    d0 = jnp.where(near, dm, 0.0).astype(BF)
    d2 = jnp.where(near, 0.0, dm).astype(BF)
    dq_t = dot(k0.T, d0, 1, 0) + dot(k1.T, d1, 1, 0) + dot(k2.T, d2, 1, 0)
    dq = (dq_t * INV_ROOT).astype(BF).T
    g1_r[0] = (dot(d1, q, 1, 0) * INV_ROOT).astype(BF)
    g1_r[1] = dot(p1_low, do, 1, 0).astype(BF)
    g2_r[0] = (dot(d2, q, 1, 0) * INV_ROOT).astype(BF)
    g2_r[1] = dot(p2_low, do, 1, 0).astype(BF)
    dk = (dot(d0, q, 1, 0) * INV_ROOT).astype(BF)
    dv = dot(p0_low, do, 1, 0).astype(BF)
    own_r[0], oth_r[0] = dq[:TOK], dq[TOK:]
    own_r[1], oth_r[1] = dk[:TOK], dk[TOK:]
    own_r[2], oth_r[2] = dv[:TOK], dv[TOK:]


def attention(part, scalars, queries, swapped, kv_own, kv1, kv2, do):
    at = lambda rows, first: pl.BlockSpec((rows, HD), lambda h, s: (0, first + h))
    deep = lambda n, rows: pl.BlockSpec((n, rows, HD), lambda h, s: (0, 0, h))
    start = part * PART
    return call(
        attention_kernel, "attention", (PART,),
        [
            pl.BlockSpec((TOK, HD), lambda h, s: (0, s[0] * HEADS + start + h)),
            at(TOK, 2 * HEADS + start),
            at(TOK, 0),
            at(TOK, 3 * HEADS + start),
            at(TOK, PART),
            at(TOK, 4 * HEADS + start),
            at(CHIP, 0),
            at(CHIP, PART),
            at(CHIP, 0),
            at(CHIP, PART),
            at(CHIP, 0),
        ],
        [deep(4, CHIP), deep(3, TOK), deep(3, TOK), deep(2, CHIP), deep(2, CHIP)],
        [bf(4, CHIP, WIDE), bf(3, TOK, WIDE), bf(3, TOK, WIDE), bf(2, CHIP, WIDE), bf(2, CHIP, WIDE)],
        2 * 18 * CHIP * CHIP * HD * PART, 12 * 1024 * WIDE, 2 * CHIP * CHIP * PART,
    )(scalars, queries, swapped, kv_own, swapped, kv_own, swapped, kv1, kv1, kv2, kv2, do)


def weight_kernel(s_ref, up_t, *refs):
    out = refs[-1]
    for n, att in enumerate(refs[:-1]):
        total = dot(up_t[0], att[0], 1, 0)
        for i in range(1, 4):
            total = total + dot(up_t[i], att[i], 1, 0)
        total = total.reshape(32, 2, 8, WIDE)
        for half in range(2):
            out[half, :, n * WIDE : (n + 1) * WIDE] = total[:, half].reshape(256, WIDE).astype(BF)


def weight_partial(scalars, up_t, atts):
    return call(
        weight_kernel, "weight_partial", (1,),
        [whole(4, 512, CHIP)] + [whole(4, CHIP, WIDE)] * CHUNKS, whole(2, 256, HALF), bf(2, 256, HALF),
        2 * CHIP * D * HALF, 4 << 20,
    )(scalars, up_t, *atts)


def plus(*terms):
    total = terms[0].astype(F32)
    for t in terms[1:]:
        total = total + t.astype(F32)
    return total


def spread_weight(part):
    width = part.shape[-1]
    mine = lax.all_to_all(part.reshape(4, 128, width), ("yh", "yl"), 0, 0, tiled=True)
    mine = plus(*mine).astype(BF).reshape(16, 8, width)
    mine = lax.all_to_all(mine, ("z", "core"), 0, 0, tiled=True)
    mine = jnp.sum(mine.reshape(8, 2, 8, width).astype(F32), axis=0)
    return jnp.concatenate([mine[0], mine[1]], axis=1)


def shards(queries, keys_values, upstream, out_weight):
    core = lax.axis_index("core")
    chip = lax.axis_index("yl") * 8 + lax.axis_index("z")
    scalars = jnp.stack([core, chip]).astype(jnp.int32)
    q, up = queries[0], upstream[0]
    kv = jnp.swapaxes(keys_values[0], 0, 1)
    cuts = cut_pairs(scalars, kv)
    kv_own, kv_oth = cuts[::2], cuts[1::2]
    kv1 = [
        jnp.concatenate([to_chip(a, 1, False), to_chip(b, 1, True)], axis=0)
        for a, b in zip(kv_own, kv_oth)
    ]
    weights = []
    for i in range(CHUNKS):
        w = lax.dynamic_slice_in_dim(out_weight, core * HALF + i * WIDE, WIDE, 1)
        w = lax.all_to_all(jnp.broadcast_to(w, (8, 256, WIDE)), FSDP, 0, 0, tiled=True)
        weights.append(w.reshape(D, WIDE))
    swapped = to_core(cut_swap(scalars, up, q, kv))
    kv2 = [to_chip(a, 1, False) for a in kv1]
    up_both, up_t = join(scalars, up, swapped)
    up_t = lax.all_to_all(up_t, "x", 0, 0, tiled=True)

    own, got, same, cross, atts = [], [], [], [], []
    for i in range(CHUNKS):
        do = project(scalars, up_both, weights[i])
        att, mine, theirs, g1, g2 = attention(i, scalars, q, swapped, kv_own[i], kv1[i], kv2[i], do)
        back = to_chip(g2, -1, False)
        atts.append(lax.all_to_all(att, "x", 0, 0, tiled=True))
        own.append(mine)
        got.append(to_core(theirs))
        back = plus(g1, back).astype(BF)
        same.append(to_chip(back[:, :TOK], -1, False))
        cross.append(to_chip(back[:, TOK:], -1, True))
    grad_weight = spread_weight(weight_partial(scalars, up_t, atts))

    def sides(a, b):
        return jnp.where(core == 0, jnp.concatenate(a + b, -1), jnp.concatenate(b + a, -1))

    grad_q = sides([a[0] for a in own], [a[0] for a in got])
    grad_kv = sides(
        [plus(a[1:], b) for a, b in zip(own, same)], [plus(a[1:], b) for a, b in zip(got, cross)]
    ).astype(BF)
    return grad_q[None], jnp.swapaxes(grad_kv, 0, 1)[None], grad_weight


def solution(mesh):
    names = tuple(name for name, _ in SPLIT)
    fine = Mesh(mesh.devices.reshape([size for _, size in SPLIT]), names)
    return jax.shard_map(
        shards,
        mesh=fine,
        in_specs=(P(FSDP, CTX, None), P(FSDP, CTX, None, None), P(FSDP, CTX, None), P(FSDP, None)),
        out_specs=(P(FSDP, CTX, None), P(FSDP, CTX, None, None), P(CTX + FSDP, None)),
        check_vma=False,
    )
```

```python
import jax
import jax.numpy as jnp
from jax import lax
from jax.experimental import pallas as pl
from jax.experimental.pallas import tpu as pltpu
from jax.sharding import Mesh
from jax.sharding import PartitionSpec as P

SPLIT = (("yl", 2), ("z", 8), ("core", 2), ("x", 4), ("yh", 2))
CTX = ("yl", "z", "core")
FSDP = ("x", "yh")

TOK = 128
CHIP = 256
HEADS = 8
HD = 128
HALF = HEADS * HD
D = 2048
NEGATIVE = -1e30
INV_ROOT = HD**-0.5
BF = jnp.bfloat16
F32 = jnp.float32
VMEM = 56 << 20


def dot(a, b, ca, cb):
    return lax.dot_general(a, b, (((ca,), (cb,)), ((), ())), preferred_element_type=F32)


def to_chip(a, by):
    pairs = [(2 * i + core, (i + by) % 16 * 2 + core) for i in range(16) for core in range(2)]
    return lax.ppermute(a, CTX, pairs)


def to_core(a):
    return lax.ppermute(a, "core", [(0, 1), (1, 0)])


def call(body, name, grid, in_specs, out_specs, out_shape, flops, moved, exps=0):
    return pl.pallas_call(
        body,
        grid_spec=pltpu.PrefetchScalarGridSpec(
            num_scalar_prefetch=1, grid=grid, in_specs=in_specs, out_specs=out_specs
        ),
        out_shape=out_shape,
        compiler_params=pltpu.CompilerParams(vmem_limit_bytes=VMEM),
        cost_estimate=pl.CostEstimate(flops=flops, bytes_accessed=moved, transcendentals=exps),
        name=name,
    )


def whole(*shape):
    return pl.BlockSpec(shape, lambda *_: (0,) * len(shape))


def bf(*shape):
    return jax.ShapeDtypeStruct(shape, BF)


def cut_kernel(s_ref, q, kv, w, mine, theirs, w_own):
    own = s_ref[0] * HALF
    for first, out in ((own, mine), (HALF - own, theirs)):
        at = pl.ds(pl.multiple_of(first, HALF), HALF)
        out[:, :HALF] = q[:, at]
        out[:, HALF : 2 * HALF] = kv[0, :, at]
        out[:, 2 * HALF :] = kv[1, :, at]
    w_own[...] = w[:, pl.ds(pl.multiple_of(own, HALF), HALF)]


def cut(scalars, q, kv, w):
    sizes = [(TOK, 3 * HALF)] * 2 + [(256, HALF)]
    return call(
        cut_kernel, "cut", (1,), [whole(TOK, D), whole(2, TOK, D), whole(256, D)],
        [whole(*n) for n in sizes], [bf(*n) for n in sizes], 0, 4 << 20,
    )(scalars, q, kv, w)


def turn_kernel(s_ref, up_own, up_oth, out):
    turned = jnp.concatenate([up_own[...], up_oth[...]], axis=0).T.reshape(32, 4, 16, CHIP)
    for to in range(4):
        out[to] = turned[:, to].reshape(512, CHIP)


def turn(scalars, up_own, up_oth):
    return call(
        turn_kernel, "turn", (1,), [whole(TOK, D)] * 2, whole(4, 512, CHIP), bf(4, 512, CHIP), 0, 2 << 20
    )(scalars, up_own, up_oth)


def project_kernel(s_ref, up_own, up_oth, w, out):
    up = jnp.concatenate([up_own[...], up_oth[...]], axis=0)
    out[...] = dot(up, w[...], 1, 0).astype(BF)


def project(scalars, up_own, up_oth, w):
    tile = 512
    cols = lambda rows: pl.BlockSpec((rows, tile), lambda n, s: (0, n))
    return call(
        project_kernel, "project", (HALF // tile,), [whole(TOK, D), whole(TOK, D), cols(D)],
        cols(CHIP), bf(CHIP, HALF), 2 * CHIP * D * HALF, 2 * D * HALF + 3 * CHIP * D,
    )(scalars, up_own, up_oth, w)


def attention_kernel(
    s_ref, q_r, k0_r, v0_r, k1_r, v1_r, k2_r, v2_r, do_r, att_r, next_r, own_r, back_r
):
    core, chip = s_ref[0], s_ref[1]
    q, do = q_r[...], do_r[...]
    k0, v0, k1, v1, k2, v2 = k0_r[...], v0_r[...], k1_r[...], v1_r[...], k2_r[...], v2_r[...]
    key_at = (lax.broadcasted_iota(jnp.int32, (CHIP, CHIP), 0) + core * TOK) & (CHIP - 1)
    query_at = (lax.broadcasted_iota(jnp.int32, (CHIP, CHIP), 1) + core * TOK) & (CHIP - 1)
    near = key_at <= query_at
    shown = jnp.logical_or(near, chip >= 2)
    sm = jnp.where(near, dot(k0, q, 1, 1), dot(k2, q, 1, 1)) * INV_ROOT
    sm = jnp.where(shown, sm, NEGATIVE)
    s1 = jnp.where(chip >= 1, dot(k1, q, 1, 1) * INV_ROOT, NEGATIVE)
    top = jnp.maximum(jnp.max(sm, axis=0, keepdims=True), jnp.max(s1, axis=0, keepdims=True))
    em = jnp.exp(sm - top)
    e1 = jnp.exp(s1 - top)
    scale = 1.0 / (jnp.sum(em, axis=0, keepdims=True) + jnp.sum(e1, axis=0, keepdims=True))
    pm = em * scale
    p1 = e1 * scale
    p1_low = p1.astype(BF)
    p0_low = jnp.where(near, pm, 0.0).astype(BF)
    p2_low = jnp.where(near, 0.0, pm).astype(BF)
    att_t = dot(v0.T, p0_low, 1, 0) + dot(v1.T, p1_low, 1, 0) + dot(v2.T, p2_low, 1, 0)
    att_t = att_t.astype(BF)
    att = att_t.T
    for to in range(4):
        att_r[to] = att
    center = jnp.sum(do.T.astype(F32) * att_t.astype(F32), axis=0, keepdims=True)
    dm = pm * (jnp.where(near, dot(v0, do, 1, 1), dot(v2, do, 1, 1)) - center)
    d1 = (p1 * (dot(v1, do, 1, 1) - center)).astype(BF)
    d0 = jnp.where(near, dm, 0.0).astype(BF)
    d2 = jnp.where(near, 0.0, dm).astype(BF)
    dq_t = dot(k0.T, d0, 1, 0) + dot(k1.T, d1, 1, 0) + dot(k2.T, d2, 1, 0)
    dq = (dq_t * INV_ROOT).astype(BF).T
    next_r[0] = dq
    for out, at, d, p in ((next_r, 1, d0, p0_low), (own_r, 0, d1, p1_low), (back_r, 0, d2, p2_low)):
        out[at] = (dot(d, q, 1, 0) * INV_ROOT).astype(BF)
        out[at + 1] = dot(p, do, 1, 0).astype(BF)


def attention(scalars, after, own, before, do):
    at = lambda first: pl.BlockSpec((CHIP, HD), lambda h, s: (0, first * HEADS + h))
    deep = lambda n: pl.BlockSpec((n, CHIP, HD), lambda h, s: (0, 0, h))
    return call(
        attention_kernel, "attention", (HEADS,),
        [at(0), at(1), at(2), at(1), at(2), at(1), at(2), at(0)], [deep(4), deep(3), deep(2), deep(2)],
        [bf(n, CHIP, HALF) for n in (4, 3, 2, 2)],
        2 * 18 * CHIP * CHIP * HD * HEADS, 12 << 20, 2 * CHIP * CHIP * HEADS,
    )(scalars, after, after, after, own, own, before, before, do)


def weight_kernel(s_ref, up_t, att, out):
    total = dot(up_t[0], att[0], 1, 0)
    for i in range(1, 4):
        total = total + dot(up_t[i], att[i], 1, 0)
    width = total.shape[1]
    total = total.reshape(32, 2, 8, width)
    for half in range(2):
        out[half] = total[:, half].reshape(256, width).astype(BF)


def weight_partial(scalars, up_t, att):
    tile = 512
    return call(
        weight_kernel, "weight_partial", (HALF // tile,),
        [whole(4, 512, CHIP), pl.BlockSpec((4, CHIP, tile), lambda n, s: (0, 0, n))],
        pl.BlockSpec((2, 256, tile), lambda n, s: (0, 0, n)), bf(2, 256, HALF),
        2 * CHIP * D * HALF, 4 << 20,
    )(scalars, up_t, att)


def plus(*terms):
    total = terms[0].astype(F32)
    for t in terms[1:]:
        total = total + t.astype(F32)
    return total


def spread_weight(part):
    width = part.shape[-1]
    mine = lax.all_to_all(part.reshape(4, 128, width), ("yh", "yl"), 0, 0, tiled=True)
    mine = plus(*mine).astype(BF).reshape(16, 8, width)
    mine = lax.all_to_all(mine, ("z", "core"), 0, 0, tiled=True)
    mine = jnp.sum(mine.reshape(8, 2, 8, width).astype(F32), axis=0)
    return jnp.concatenate([mine[0], mine[1]], axis=1)


def shards(queries, keys_values, upstream, out_weight):
    core = lax.axis_index("core")
    chip = (lax.axis_index("yl") * 8 + lax.axis_index("z") + 1) & 15
    scalars = jnp.stack([core, chip]).astype(jnp.int32)

    up_own = to_chip(upstream[0], -1)
    kv = jnp.swapaxes(keys_values[0], 0, 1)
    mine, theirs, w = cut(scalars, queries[0], kv, out_weight)
    mine = jnp.concatenate([mine, to_core(theirs)], axis=0)
    after, before = to_chip(mine, -1), to_chip(mine, 1)
    w = lax.all_to_all(jnp.broadcast_to(w, (8,) + w.shape), FSDP, 0, 0, tiled=True).reshape(D, HALF)
    up_oth = to_core(up_own)
    up_t = lax.all_to_all(turn(scalars, up_own, up_oth), "x", 0, 0, tiled=True)

    do = project(scalars, up_own, up_oth, w)
    att, on, own, back = attention(scalars, after, mine, before, do)
    on, back = to_chip(on, 1), to_chip(back, -1)
    att = lax.all_to_all(att, "x", 0, 0, tiled=True)
    grad_weight = spread_weight(weight_partial(scalars, up_t, att))

    on = jnp.concatenate([on[:1], plus(on[1:], own, back).astype(BF)], axis=0)
    mine, theirs = on[:, :TOK], to_core(on[:, TOK:])
    grads = jnp.where(core == 0, jnp.concatenate([mine, theirs], -1), jnp.concatenate([theirs, mine], -1))
    return grads[:1], jnp.swapaxes(grads[1:], 0, 1)[None], grad_weight


def solution(mesh):
    names = tuple(name for name, _ in SPLIT)
    fine = Mesh(mesh.devices.reshape([size for _, size in SPLIT]), names)
    return jax.shard_map(
        shards,
        mesh=fine,
        in_specs=(P(FSDP, CTX, None), P(FSDP, CTX, None, None), P(FSDP, CTX, None), P(FSDP, None)),
        out_specs=(P(FSDP, CTX, None), P(FSDP, CTX, None, None), P(CTX + FSDP, None)),
        check_vma=False,
    )
```

```python
import jax
import jax.numpy as jnp
from jax import lax
from jax.experimental import pallas as pl
from jax.experimental.pallas import tpu as pltpu
from jax.sharding import Mesh
from jax.sharding import PartitionSpec as P

SPLIT = (("yl", 2), ("z", 8), ("core", 2), ("x", 4), ("yh", 2))
CTX = ("yl", "z", "core")
FSDP = ("x", "yh")

TOK = 128
CHIP = 256
HEADS = 8
HD = 128
HALF = HEADS * HD
D = 2048
NEGATIVE = -1e30
INV_ROOT = HD**-0.5
BF = jnp.bfloat16
F32 = jnp.float32
VMEM = {"cut": 56, "project": 56, "forward": 56, "backward": 56, "weight_partial": 56, "finish": 56, "add_y": 56}


def dot(a, b, ca, cb):
    return lax.dot_general(a, b, (((ca,), (cb,)), ((), ())), preferred_element_type=F32)


def to_chip(a, by):
    pairs = [(2 * i + core, (i + by) % 16 * 2 + core) for i in range(16) for core in range(2)]
    return lax.ppermute(a, CTX, pairs)


def to_core(a):
    return lax.ppermute(a, "core", [(0, 1), (1, 0)])


def to_x(a, by):
    return lax.ppermute(a, "x", [(i, (i + by) % 4) for i in range(4)])


def to_y_neighbour(a):
    return lax.ppermute(a, ("yl", "yh"), [(0, 3), (3, 0), (1, 2), (2, 1)])


def call(body, name, grid, in_specs, out_specs, out_shape, flops, moved, exps=0):
    return pl.pallas_call(
        body,
        grid_spec=pltpu.PrefetchScalarGridSpec(
            num_scalar_prefetch=1, grid=grid, in_specs=in_specs, out_specs=out_specs
        ),
        out_shape=out_shape,
        compiler_params=pltpu.CompilerParams(vmem_limit_bytes=VMEM[name] << 20),
        cost_estimate=pl.CostEstimate(flops=flops, bytes_accessed=moved, transcendentals=exps),
        name=name,
    )


AFTER = pl.BlockSpec(memory_space=pl.ANY)


def whole(*shape):
    return pl.BlockSpec(shape, lambda *_: (0,) * len(shape))


def bf(*shape):
    return jax.ShapeDtypeStruct(shape, BF)


def cut_kernel(s_ref, q, kv, w, mine, theirs, w_own):
    own = s_ref[0] * HALF
    for first, out in ((own, mine), (HALF - own, theirs)):
        at = pl.ds(pl.multiple_of(first, HALF), HALF)
        out[:, :HALF] = q[:, at]
        out[:, HALF : 2 * HALF] = kv[0, :, at]
        out[:, 2 * HALF :] = kv[1, :, at]
    w_own[...] = w[:, pl.ds(pl.multiple_of(own, HALF), HALF)]


def cut(scalars, q, kv, w):
    sizes = [(TOK, 3 * HALF)] * 2 + [(256, HALF)]
    return call(
        cut_kernel, "cut", (1,), [whole(TOK, D), whole(2, TOK, D), whole(256, D)],
        [whole(*n) for n in sizes], [bf(*n) for n in sizes], 0, 4 << 20,
    )(scalars, q, kv, w)


def project_kernel(s_ref, up_own, up_oth, w0, w1, w3, wa, wb, out):
    x, yh = s_ref[2], s_ref[3]
    total = None
    pieces = [(0, 0, w0, 0), (0, 1, w0, 256), (1, 0, w1, 0), (1, 1, w1, 256)]
    pieces += [(3, 0, w3, 0), (3, 1, w3, 256), (2, 0, wa, 0), (2, 1, wb, 0)]
    for dx, dy, ref, start in pieces:
        block = ((x + dx) & 3) * 2 + ((yh + dy) & 1)
        at = pl.ds(pl.multiple_of(block * 256, 256), 256)
        left = jnp.concatenate([up_own[:, at], up_oth[:, at]], axis=0)
        part = dot(left, ref[start : start + 256, :], 1, 0)
        total = part if total is None else total + part
    out[...] = total.astype(BF)


def project(scalars, up_own, up_oth, *ws):
    tile = 512
    cols = lambda rows: pl.BlockSpec((rows, tile), lambda n, s: (0, n))
    return call(
        project_kernel, "project", (HALF // tile,),
        [whole(TOK, D), whole(TOK, D), cols(512), cols(512), cols(512), cols(256), cols(256)],
        cols(CHIP), bf(CHIP, HALF), 2 * CHIP * D * HALF, 2 * D * HALF + 3 * CHIP * D,
    )(scalars, up_own, up_oth, *ws)


def scores(s_ref, q, k0, k1, k2):
    core, chip = s_ref[0], s_ref[1]
    key_at = (lax.broadcasted_iota(jnp.int32, (CHIP, CHIP), 0) + core * TOK) & (CHIP - 1)
    query_at = (lax.broadcasted_iota(jnp.int32, (CHIP, CHIP), 1) + core * TOK) & (CHIP - 1)
    near = key_at <= query_at
    shown = jnp.logical_or(near, chip >= 2)
    sm = jnp.where(near, dot(k0, q, 1, 1), dot(k2, q, 1, 1)) * INV_ROOT
    sm = jnp.where(shown, sm, NEGATIVE)
    s1 = jnp.where(chip >= 1, dot(k1, q, 1, 1) * INV_ROOT, NEGATIVE)
    return near, sm, s1


def split(near, pm):
    return jnp.where(near, pm, 0.0).astype(BF), jnp.where(near, 0.0, pm).astype(BF)


def forward_kernel(s_ref, wa_ref, wb_ref, q_r, k0_r, v0_r, k1_r, v1_r, k2_r, v2_r, up_own, up_oth, out_r, log_r):
    near, sm, s1 = scores(s_ref, q_r[...], k0_r[...], k1_r[...], k2_r[...])
    top = jnp.maximum(jnp.max(sm, axis=0, keepdims=True), jnp.max(s1, axis=0, keepdims=True))
    em = jnp.exp(sm - top)
    e1 = jnp.exp(s1 - top)
    total = jnp.sum(em, axis=0, keepdims=True) + jnp.sum(e1, axis=0, keepdims=True)
    log_r[0] = top + jnp.log(total)
    scale = 1.0 / total
    p0, p2 = split(near, em * scale)
    p1 = (e1 * scale).astype(BF)
    att = dot(v0_r[...].T, p0, 1, 0) + dot(v1_r[...].T, p1, 1, 0) + dot(v2_r[...].T, p2, 1, 0)
    att = att.astype(BF).T
    up = jnp.where((pl.program_id(0) & 1) == 0, up_own[...], up_oth[...])
    turned = up.T.reshape(8, 4, 16, TOK)
    for to in range(4):
        out_r[to, :CHIP] = att
        out_r[to, CHIP:] = turned[:, to].reshape(TOK, TOK)


def at(first):
    return pl.BlockSpec((CHIP, HD), lambda h, s: (0, first * HEADS + h))


def forward(scalars, wa, wb, after, own, before, up_own, up_oth):
    quarter = pl.BlockSpec((TOK, 512), lambda h, s: (0, h // 2))
    return call(
        forward_kernel, "forward", (HEADS,),
        [AFTER, AFTER, at(0), at(1), at(2), at(1), at(2), at(1), at(2), quarter, quarter],
        [
            pl.BlockSpec((4, CHIP + TOK, HD), lambda h, s: (0, 0, h)),
            pl.BlockSpec((1, 1, CHIP), lambda h, s: (h, 0, 0)),
        ],
        [bf(4, CHIP + TOK, HALF), jax.ShapeDtypeStruct((HEADS, 1, CHIP), F32)],
        2 * 6 * CHIP * CHIP * HD * HEADS, 6 << 20, 2 * CHIP * CHIP * HEADS,
    )(scalars, wa, wb, after, after, after, own, own, before, before, up_own, up_oth)


def backward_kernel(
    s_ref, q_r, k0_r, v0_r, k1_r, v1_r, k2_r, v2_r, do_r, att_r, log_r, next_r, own_r, back_r
):
    q, do = q_r[...], do_r[...]
    k0, k1, k2 = k0_r[...], k1_r[...], k2_r[...]
    near, sm, s1 = scores(s_ref, q, k0, k1, k2)
    pm = jnp.exp(sm - log_r[0])
    p1 = jnp.exp(s1 - log_r[0])
    p0_low, p2_low = split(near, pm)
    p1_low = p1.astype(BF)
    center = jnp.sum((do.astype(F32) * att_r[0].astype(F32)).T, axis=0, keepdims=True)
    dm = pm * (jnp.where(near, dot(v0_r[...], do, 1, 1), dot(v2_r[...], do, 1, 1)) - center)
    d1 = (p1 * (dot(v1_r[...], do, 1, 1) - center)).astype(BF)
    d0, d2 = split(near, dm)
    dq = dot(k0.T, d0, 1, 0) + dot(k1.T, d1, 1, 0) + dot(k2.T, d2, 1, 0)
    next_r[0] = (dq * INV_ROOT).astype(BF).T
    for out, first, d, p in ((next_r, 1, d0, p0_low), (own_r, 0, d1, p1_low), (back_r, 0, d2, p2_low)):
        out[first] = (dot(d, q, 1, 0) * INV_ROOT).astype(BF)
        out[first + 1] = dot(p, do, 1, 0).astype(BF)


def backward(scalars, after, own, before, do, sent, log):
    deep = lambda n: pl.BlockSpec((n, CHIP, HD), lambda h, s: (0, 0, h))
    return call(
        backward_kernel, "backward", (HEADS,),
        [at(0), at(1), at(2), at(1), at(2), at(1), at(2), at(0)]
        + [deep(1), pl.BlockSpec((1, 1, CHIP), lambda h, s: (h, 0, 0))],
        [deep(3), deep(2), deep(2)], [bf(n, CHIP, HALF) for n in (3, 2, 2)],
        2 * 15 * CHIP * CHIP * HD * HEADS, 12 << 20, 2 * CHIP * CHIP * HEADS,
    )(scalars, after, after, after, own, own, before, before, do, sent, log)


def weight_kernel(s_ref, got, out):
    for n in range(HALF // 512):
        cols = slice(512 * n, 512 * (n + 1))
        for b in range(4):
            total = None
            for i in range(4):
                part = dot(got[i, CHIP:, b * CHIP : (b + 1) * CHIP], got[i, :CHIP, cols], 1, 0)
                total = part if total is None else total + part
            total = total.reshape(8, 2, 8, 512)
            for half in range(2):
                out[half, 64 * b : 64 * (b + 1), cols] = total[:, half].reshape(64, 512).astype(BF)


def weight_partial(scalars, got):
    return call(
        weight_kernel, "weight_partial", (1,), [whole(4, CHIP + TOK, HALF)], whole(2, 256, HALF), bf(2, 256, HALF),
        2 * CHIP * D * HALF, 4 << 20,
    )(scalars, got)


def plus(*terms):
    total = terms[0].astype(F32)
    for t in terms[1:]:
        total = total + t.astype(F32)
    return total


def finish_kernel(s_ref, part_ref, on, own, back, mine, theirs):
    for out, rows in ((mine, slice(0, TOK)), (theirs, slice(TOK, CHIP))):
        out[0] = on[0, rows]
        for i in range(2):
            out[1 + i] = plus(on[1 + i, rows], own[i, rows], back[i, rows]).astype(BF)


def finish(scalars, part, on, own, back):
    tile = 256
    deep = lambda n, rows: pl.BlockSpec((n, rows, tile), lambda i, s: (0, 0, i))
    return call(
        finish_kernel, "finish", (HALF // tile,), [AFTER, deep(3, CHIP), deep(2, CHIP), deep(2, CHIP)],
        [deep(3, TOK)] * 2, [bf(3, TOK, HALF)] * 2, 0, 5 << 20,
    )(scalars, part, on, own, back)


def add_kernel(s_ref, back_ref, parts, out):
    out[...] = plus(*[parts[i] for i in range(4)]).astype(BF)


def sum_over_y(scalars, part, back):
    parts = lax.all_to_all(part.reshape(4, 128, HALF), ("yh", "yl"), 0, 0, tiled=True)
    return call(
        add_kernel, "add_y", (1,), [AFTER, whole(4, 128, HALF)], whole(128, HALF), bf(128, HALF), 0, 2 << 20
    )(scalars, back, parts)


def sum_over_z(part):
    mine = lax.all_to_all(part.reshape(16, 8, HALF), ("z", "core"), 0, 0, tiled=True)
    mine = jnp.sum(mine.reshape(8, 2, 8, HALF).astype(F32), axis=0)
    return jnp.concatenate([mine[0], mine[1]], axis=1)


def shards(queries, keys_values, upstream, out_weight):
    core = lax.axis_index("core")
    x, yh = lax.axis_index("x"), lax.axis_index("yh")
    chip = (lax.axis_index("yl") * 8 + lax.axis_index("z") + 1) & 15
    scalars = jnp.stack([core, chip, x, yh]).astype(jnp.int32)

    up_own = to_chip(upstream[0], -1)
    kv = jnp.swapaxes(keys_values[0], 0, 1)
    mine, theirs, w = cut(scalars, queries[0], kv, out_weight)
    mine = jnp.concatenate([mine, to_core(theirs)], axis=0)
    after, before = to_chip(mine, -1), to_chip(mine, 1)
    w0 = jnp.concatenate([w, to_y_neighbour(w)], axis=0)
    w3, w1 = to_x(w0, 1), to_x(w0, -1)
    wa, wb = to_x(w3[:256], 1), to_x(w1[256:], -1)
    up_oth = to_core(up_own)

    sent, log = forward(scalars, wa, wb, after, mine, before, up_own, up_oth)
    got = lax.all_to_all(sent, "x", 0, 0, tiled=True)
    do = project(scalars, up_own, up_oth, w0, w1, w3, wa, wb)
    on, own, back = backward(scalars, after, mine, before, do, sent, log)
    on, back = to_chip(on, 1), to_chip(back, -1)
    part = sum_over_y(scalars, weight_partial(scalars, got), back)
    grad_weight = sum_over_z(part)
    mine, theirs = finish(scalars, part, on, own, back)
    theirs = to_core(theirs)
    grads = jnp.where(core == 0, jnp.concatenate([mine, theirs], -1), jnp.concatenate([theirs, mine], -1))
    return grads[:1], jnp.swapaxes(grads[1:], 0, 1)[None], grad_weight


def solution(mesh):
    names = tuple(name for name, _ in SPLIT)
    fine = Mesh(mesh.devices.reshape([size for _, size in SPLIT]), names)
    return jax.shard_map(
        shards,
        mesh=fine,
        in_specs=(P(FSDP, CTX, None), P(FSDP, CTX, None, None), P(FSDP, CTX, None), P(FSDP, None)),
        out_specs=(P(FSDP, CTX, None), P(FSDP, CTX, None, None), P(CTX + FSDP, None)),
        check_vma=False,
    )
```

```python
import jax
import jax.numpy as jnp
from jax import lax
from jax.experimental import pallas as pl
from jax.experimental.pallas import tpu as pltpu
from jax.sharding import Mesh
from jax.sharding import PartitionSpec as P

SPLIT = (("yl", 2), ("z", 8), ("core", 2), ("x", 4), ("yh", 2))
CTX = ("yl", "z", "core")
FSDP = ("x", "yh")

TOK = 128
CHIP = 256
HEADS = 8
HD = 128
HALF = HEADS * HD
D = 2048
NEGATIVE = -1e30
INV_ROOT = HD**-0.5
BF = jnp.bfloat16
F32 = jnp.float32
VMEM = {"cut": 56, "project": 56, "forward": 56, "backward": 56, "weight_partial": 56, "finish": 56, "pack": 8, "turn": 8, "add_y": 8}


def dot(a, b, ca, cb):
    return lax.dot_general(a, b, (((ca,), (cb,)), ((), ())), preferred_element_type=F32)


def to_chip(a, by, cross=False):
    pairs = []
    for i in range(16):
        for core in range(2):
            pairs.append((2 * i + core, (i + by) % 16 * 2 + (1 - core if cross else core)))
    return lax.ppermute(a, CTX, pairs)


def to_core(a):
    return lax.ppermute(a, "core", [(0, 1), (1, 0)])


def to_x(a, by):
    return lax.ppermute(a, "x", [(i, (i + by) % 4) for i in range(4)])


def to_y_neighbour(a):
    return lax.ppermute(a, ("yl", "yh"), [(0, 3), (3, 0), (1, 2), (2, 1)])


def call(body, name, grid, in_specs, out_specs, out_shape, flops, moved, exps=0):
    return pl.pallas_call(
        body,
        grid_spec=pltpu.PrefetchScalarGridSpec(
            num_scalar_prefetch=1, grid=grid, in_specs=in_specs, out_specs=out_specs
        ),
        out_shape=out_shape,
        compiler_params=pltpu.CompilerParams(vmem_limit_bytes=VMEM[name] << 20),
        cost_estimate=pl.CostEstimate(flops=flops, bytes_accessed=moved, transcendentals=exps),
        name=name,
    )


AFTER = pl.BlockSpec(memory_space=pl.ANY)


def whole(*shape):
    return pl.BlockSpec(shape, lambda *_: (0,) * len(shape))


def bf(*shape):
    return jax.ShapeDtypeStruct(shape, BF)


def cut_kernel(s_ref, q, kv, w, mine, theirs, w_own):
    own = s_ref[0] * HALF
    for first, out in ((own, mine), (HALF - own, theirs)):
        at = pl.ds(pl.multiple_of(first, HALF), HALF)
        out[:, :HALF] = q[:, at]
        out[:, HALF : 2 * HALF] = kv[0, :, at]
        out[:, 2 * HALF :] = kv[1, :, at]
    w_own[...] = w[:, pl.ds(pl.multiple_of(own, HALF), HALF)]


def cut(scalars, q, kv, w):
    sizes = [(TOK, 3 * HALF)] * 2 + [(256, HALF)]
    return call(
        cut_kernel, "cut", (1,), [whole(TOK, D), whole(2, TOK, D), whole(256, D)],
        [whole(*n) for n in sizes], [bf(*n) for n in sizes], 0, 4 << 20,
    )(scalars, q, kv, w)


def pack_kernel(s_ref, first_ref, mine, got, out):
    out[:TOK] = mine[...]
    out[TOK:] = got[...]


def pack(scalars, first, mine, got):
    tile = HALF
    part = lambda rows: pl.BlockSpec((rows, tile), lambda n, s: (0, n))
    return call(
        pack_kernel, "pack", (3,), [AFTER, part(TOK), part(TOK)], part(CHIP), bf(CHIP, 3 * HALF), 0, 3 << 20
    )(scalars, first, mine, got)


def turn_kernel(s_ref, up_own, up_oth, out):
    for i, up in enumerate((up_own, up_oth)):
        turned = up[...].T.reshape(8, 4, 16, TOK)
        for to in range(4):
            out[to, :, i * TOK : (i + 1) * TOK] = turned[:, to].reshape(TOK, TOK)


def turn(scalars, up_own, up_oth):
    quarter = pl.BlockSpec((TOK, 512), lambda b, s: (0, b))
    return call(
        turn_kernel, "turn", (4,), [quarter] * 2, pl.BlockSpec((4, TOK, CHIP), lambda b, s: (0, 0, b)),
        bf(4, TOK, HALF), 0, 2 << 20,
    )(scalars, up_own, up_oth)


def project_kernel(s_ref, up_own, up_oth, w0, w1, w3, wa, wb, out):
    x, yh = s_ref[2], s_ref[3]
    total = None
    pieces = [(0, 0, w0, 0), (0, 1, w0, 256), (1, 0, w1, 0), (1, 1, w1, 256)]
    pieces += [(3, 0, w3, 0), (3, 1, w3, 256), (2, 0, wa, 0), (2, 1, wb, 0)]
    for dx, dy, ref, start in pieces:
        block = ((x + dx) & 3) * 2 + ((yh + dy) & 1)
        at = pl.ds(pl.multiple_of(block * 256, 256), 256)
        left = jnp.concatenate([up_own[:, at], up_oth[:, at]], axis=0)
        part = dot(left, ref[start : start + 256, :], 1, 0)
        total = part if total is None else total + part
    out[...] = total.astype(BF)


def project(scalars, up_own, up_oth, *ws):
    tile = 512
    cols = lambda rows: pl.BlockSpec((rows, tile), lambda n, s: (0, n))
    return call(
        project_kernel, "project", (HALF // tile,),
        [whole(TOK, D), whole(TOK, D), cols(512), cols(512), cols(512), cols(256), cols(256)],
        cols(CHIP), bf(CHIP, HALF), 2 * CHIP * D * HALF, 2 * D * HALF + 3 * CHIP * D,
    )(scalars, up_own, up_oth, *ws)


def scores(s_ref, q, k0, k1, k2):
    core, chip = s_ref[0], s_ref[1]
    key_at = (lax.broadcasted_iota(jnp.int32, (CHIP, CHIP), 0) + core * TOK) & (CHIP - 1)
    query_at = (lax.broadcasted_iota(jnp.int32, (CHIP, CHIP), 1) + core * TOK) & (CHIP - 1)
    near = key_at <= query_at
    shown = jnp.logical_or(near, chip >= 2)
    sm = jnp.where(near, dot(k0, q, 1, 1), dot(k2, q, 1, 1)) * INV_ROOT
    sm = jnp.where(shown, sm, NEGATIVE)
    s1 = jnp.where(chip >= 1, dot(k1, q, 1, 1) * INV_ROOT, NEGATIVE)
    return near, sm, s1


def split(near, pm):
    return jnp.where(near, pm, 0.0).astype(BF), jnp.where(near, 0.0, pm).astype(BF)


def forward_kernel(s_ref, wa_ref, wb_ref, q_r, k0_r, v0_r, k1_r, v1_r, k2_r, v2_r, up_t, out_r, log_r):
    near, sm, s1 = scores(s_ref, q_r[...], k0_r[...], k1_r[...], k2_r[...])
    top = jnp.maximum(jnp.max(sm, axis=0, keepdims=True), jnp.max(s1, axis=0, keepdims=True))
    em = jnp.exp(sm - top)
    e1 = jnp.exp(s1 - top)
    total = jnp.sum(em, axis=0, keepdims=True) + jnp.sum(e1, axis=0, keepdims=True)
    log_r[0] = top + jnp.log(total)
    scale = 1.0 / total
    p0, p2 = split(near, em * scale)
    p1 = (e1 * scale).astype(BF)
    att = dot(v0_r[...].T, p0, 1, 0) + dot(v1_r[...].T, p1, 1, 0) + dot(v2_r[...].T, p2, 1, 0)
    att = att.astype(BF).T
    for to in range(4):
        out_r[to, :CHIP] = att
        out_r[to, CHIP:] = up_t[to]


def at(first):
    return pl.BlockSpec((CHIP, HD), lambda h, s: (0, first * HEADS + h))


def forward(scalars, wa, wb, after, own, before, up_t):
    return call(
        forward_kernel, "forward", (HEADS,),
        [AFTER, AFTER, at(0), at(1), at(2), at(1), at(2), at(1), at(2)]
        + [pl.BlockSpec((4, TOK, HD), lambda h, s: (0, 0, h))],
        [
            pl.BlockSpec((4, CHIP + TOK, HD), lambda h, s: (0, 0, h)),
            pl.BlockSpec((1, 1, CHIP), lambda h, s: (h, 0, 0)),
        ],
        [bf(4, CHIP + TOK, HALF), jax.ShapeDtypeStruct((HEADS, 1, CHIP), F32)],
        2 * 6 * CHIP * CHIP * HD * HEADS, 6 << 20, 2 * CHIP * CHIP * HEADS,
    )(scalars, wa, wb, after, after, after, own, own, before, before, up_t)


def backward_kernel(
    s_ref, q_r, k0_r, v0_r, k1_r, v1_r, k2_r, v2_r, do_r, att_r, log_r,
    on_same, on_cross, own_same, own_cross, back_same, back_cross,
):
    q, do = q_r[...], do_r[...]
    k0, k1, k2 = k0_r[...], k1_r[...], k2_r[...]
    near, sm, s1 = scores(s_ref, q, k0, k1, k2)
    pm = jnp.exp(sm - log_r[0])
    p1 = jnp.exp(s1 - log_r[0])
    p0_low, p2_low = split(near, pm)
    p1_low = p1.astype(BF)
    center = jnp.sum((do.astype(F32) * att_r[0].astype(F32)).T, axis=0, keepdims=True)
    dm = pm * (jnp.where(near, dot(v0_r[...], do, 1, 1), dot(v2_r[...], do, 1, 1)) - center)
    d1 = (p1 * (dot(v1_r[...], do, 1, 1) - center)).astype(BF)
    d0, d2 = split(near, dm)
    dq = dot(k0.T, d0, 1, 0) + dot(k1.T, d1, 1, 0) + dot(k2.T, d2, 1, 0)
    dq = (dq * INV_ROOT).astype(BF).T
    on_same[0], on_cross[0] = dq[:TOK], dq[TOK:]
    for same, cross, first, d, p in (
        (on_same, on_cross, 1, d0, p0_low), (own_same, own_cross, 0, d1, p1_low), (back_same, back_cross, 0, d2, p2_low)
    ):
        dk = (dot(d, q, 1, 0) * INV_ROOT).astype(BF)
        dv = dot(p, do, 1, 0).astype(BF)
        same[first], cross[first] = dk[:TOK], dk[TOK:]
        same[first + 1], cross[first + 1] = dv[:TOK], dv[TOK:]


def backward(scalars, after, own, before, do, sent, log):
    return call(
        backward_kernel, "backward", (HEADS,),
        [at(0), at(1), at(2), at(1), at(2), at(1), at(2), at(0)]
        + [pl.BlockSpec((1, CHIP, HD), lambda h, s: (0, 0, h)), pl.BlockSpec((1, 1, CHIP), lambda h, s: (h, 0, 0))],
        [pl.BlockSpec((n, TOK, HD), lambda h, s: (0, 0, h)) for n in (3, 3, 2, 2, 2, 2)],
        [bf(n, TOK, HALF) for n in (3, 3, 2, 2, 2, 2)],
        2 * 15 * CHIP * CHIP * HD * HEADS, 12 << 20, 2 * CHIP * CHIP * HEADS,
    )(scalars, after, after, after, own, own, before, before, do, sent, log)


def weight_kernel(s_ref, on_ref, own_ref, back_s_ref, back_x_ref, up_t, att, out):
    width = att.shape[2]
    for b in range(4):
        total = None
        for i in range(4):
            part = dot(up_t[i, CHIP:, b * CHIP : (b + 1) * CHIP], att[i], 1, 0)
            total = part if total is None else total + part
        total = total.reshape(8, 2, 8, width)
        for half in range(2):
            out[half, 64 * b : 64 * (b + 1)] = total[:, half].reshape(64, width).astype(BF)


def weight_partial(scalars, got, *sent):
    tile = 256
    return call(
        weight_kernel, "weight_partial", (HALF // tile,),
        [AFTER] * 4 + [whole(4, CHIP + TOK, HALF), pl.BlockSpec((4, CHIP, tile), lambda n, s: (0, 0, n))],
        pl.BlockSpec((2, 256, tile), lambda n, s: (0, 0, n)), bf(2, 256, HALF),
        2 * CHIP * D * HALF, 4 << 20,
    )(scalars, *sent, got, got)


def plus(*terms):
    total = terms[0].astype(F32)
    for t in terms[1:]:
        total = total + t.astype(F32)
    return total


def finish_kernel(s_ref, part_ref, on_s, on_x, own_s, own_x, back_s, back_x, out):
    side = pl.program_id(0)
    for here, on, own, back in ((0, on_s, own_s, back_s), (1, on_x, own_x, back_x)):

        @pl.when(side == here)
        def _():
            out[0] = on[0]
            for i in range(2):
                out[1 + i] = plus(on[1 + i], own[i], back[i]).astype(BF)


def finish(scalars, part, *terms):
    tile = 512
    tiles = HALF // tile
    same = lambda n: pl.BlockSpec((n, TOK, tile), lambda i, j, s: (0, 0, jnp.where(i == 0, j, tiles - 1)))
    cross = lambda n: pl.BlockSpec((n, TOK, tile), lambda i, j, s: (0, 0, jnp.where(i == 0, 0, j)))
    return call(
        finish_kernel, "finish", (2, tiles), [AFTER] + [f(n) for n in (3, 2, 2) for f in (same, cross)],
        pl.BlockSpec((3, TOK, tile), lambda i, j, s: (0, 0, ((s[0] + i) & 1) * tiles + j)), bf(3, TOK, D), 0, 5 << 20,
    )(scalars, part, *terms)


def add_kernel(s_ref, on_ref, parts, out):
    out[...] = plus(*[parts[i] for i in range(4)]).astype(BF)


def sum_over_y(scalars, part, sent):
    parts = lax.all_to_all(part.reshape(4, 128, HALF), ("yh", "yl"), 0, 0, tiled=True)
    return call(
        add_kernel, "add_y", (1,), [AFTER, whole(4, 128, HALF)], whole(128, HALF), bf(128, HALF), 0, 2 << 20
    )(scalars, sent, parts)


def sum_over_z(part):
    mine = lax.all_to_all(part.reshape(16, 8, HALF), ("z", "core"), 0, 0, tiled=True)
    mine = jnp.sum(mine.reshape(8, 2, 8, HALF).astype(F32), axis=0)
    return jnp.concatenate([mine[0], mine[1]], axis=1)


def shards(queries, keys_values, upstream, out_weight):
    core = lax.axis_index("core")
    x, yh = lax.axis_index("x"), lax.axis_index("yh")
    chip = (lax.axis_index("yl") * 8 + lax.axis_index("z") + 1) & 15
    scalars = jnp.stack([core, chip, x, yh]).astype(jnp.int32)

    up_own = to_chip(upstream[0], -1)
    kv = jnp.swapaxes(keys_values[0], 0, 1)
    mine, theirs, w = cut(scalars, queries[0], kv, out_weight)
    mine = pack(scalars, up_own, mine, to_core(theirs))
    after, before = to_chip(mine, -1), to_chip(mine, 1)
    w0 = jnp.concatenate([w, to_y_neighbour(w)], axis=0)
    w3, w1 = to_x(w0, 1), to_x(w0, -1)
    wa, wb = to_x(w3[:256], 1), to_x(w1[256:], -1)
    up_oth = to_core(up_own)
    up_t = turn(scalars, up_own, up_oth)

    sent, log = forward(scalars, wa, wb, after, mine, before, up_t)
    got = lax.all_to_all(sent, "x", 0, 0, tiled=True)
    do = project(scalars, up_own, up_oth, w0, w1, w3, wa, wb)
    on_s, on_x, own_s, own_x, back_s, back_x = backward(scalars, after, mine, before, do, sent, log)
    on_s, on_x = to_chip(on_s, 1), to_chip(on_x, 1, True)
    back_s, back_x = to_chip(back_s, -1), to_chip(back_x, -1, True)
    own_x = to_core(own_x)
    part = weight_partial(scalars, got, on_s, own_x, back_s, back_x)
    part = sum_over_y(scalars, part, on_x)
    grads = finish(scalars, part, on_s, on_x, own_s, own_x, back_s, back_x)
    return grads[:1], jnp.swapaxes(grads[1:], 0, 1)[None], sum_over_z(part)


def solution(mesh):
    names = tuple(name for name, _ in SPLIT)
    fine = Mesh(mesh.devices.reshape([size for _, size in SPLIT]), names)
    return jax.shard_map(
        shards,
        mesh=fine,
        in_specs=(P(FSDP, CTX, None), P(FSDP, CTX, None, None), P(FSDP, CTX, None), P(FSDP, None)),
        out_specs=(P(FSDP, CTX, None), P(FSDP, CTX, None, None), P(CTX + FSDP, None)),
        check_vma=False,
    )
```

```python
import jax
import jax.numpy as jnp
from jax import lax
from jax.experimental import pallas as pl
from jax.experimental.pallas import tpu as pltpu
from jax.sharding import Mesh
from jax.sharding import PartitionSpec as P

SPLIT = (("yl", 2), ("z", 8), ("core", 2), ("x", 4), ("yh", 2))
CTX = ("yl", "z", "core")
FSDP = ("x", "yh")

TOK = 128
CHIP = 256
HEADS = 8
HD = 128
HALF = HEADS * HD
D = 2048
TOGETHER = 2
STEPS = HEADS // TOGETHER
WIDE = TOGETHER * HD
NEGATIVE = -1e30
INV_ROOT = HD**-0.5
BF = jnp.bfloat16
F32 = jnp.float32
VMEM = {"cut": 56, "project": 56, "forward": 56, "backward": 56, "weight_partial": 56, "finish": 56, "pack": 8, "turn": 8, "add_y": 8}


def dot(a, b, ca, cb):
    return lax.dot_general(a, b, (((ca,), (cb,)), ((), ())), preferred_element_type=F32)


def to_chip(a, by, cross=False):
    pairs = []
    for i in range(16):
        for core in range(2):
            pairs.append((2 * i + core, (i + by) % 16 * 2 + (1 - core if cross else core)))
    return lax.ppermute(a, CTX, pairs)


def to_core(a):
    return lax.ppermute(a, "core", [(0, 1), (1, 0)])


def to_x(a, by):
    return lax.ppermute(a, "x", [(i, (i + by) % 4) for i in range(4)])


def to_y_neighbour(a):
    return lax.ppermute(a, ("yl", "yh"), [(0, 3), (3, 0), (1, 2), (2, 1)])


def call(body, name, grid, in_specs, out_specs, out_shape, flops, moved, exps=0):
    return pl.pallas_call(
        body,
        grid_spec=pltpu.PrefetchScalarGridSpec(
            num_scalar_prefetch=1, grid=grid, in_specs=in_specs, out_specs=out_specs
        ),
        out_shape=out_shape,
        compiler_params=pltpu.CompilerParams(vmem_limit_bytes=VMEM[name] << 20),
        cost_estimate=pl.CostEstimate(flops=flops, bytes_accessed=moved, transcendentals=exps),
        name=name,
    )


AFTER = pl.BlockSpec(memory_space=pl.ANY)


def whole(*shape):
    return pl.BlockSpec(shape, lambda *_: (0,) * len(shape))


def bf(*shape):
    return jax.ShapeDtypeStruct(shape, BF)


def cut_kernel(s_ref, q, kv, mine, theirs):
    own = s_ref[0] * HALF
    for first, out in ((own, mine), (HALF - own, theirs)):
        at = pl.ds(pl.multiple_of(first, HALF), HALF)
        out[:, :HALF] = q[:, at]
        out[:, HALF : 2 * HALF] = kv[0, :, at]
        out[:, 2 * HALF :] = kv[1, :, at]


def cut(scalars, q, kv):
    return call(
        cut_kernel, "cut", (1,), [whole(TOK, D), whole(2, TOK, D)], [whole(TOK, 3 * HALF)] * 2,
        [bf(TOK, 3 * HALF)] * 2, 0, 4 << 20,
    )(scalars, q, kv)


def pack_kernel(s_ref, *refs):
    mine, got, out = refs[-3:]
    rows = mine.shape[0]
    out[:rows] = mine[...]
    out[rows:] = got[...]


def pack(scalars, mine, got, *first):
    rows, width = mine.shape
    part = lambda n: pl.BlockSpec((n, HALF), lambda i, s: (0, i))
    return call(
        pack_kernel, "pack", (width // HALF,), [AFTER] * len(first) + [part(rows)] * 2, part(2 * rows),
        bf(2 * rows, width), 0, 8 * rows * width,
    )(scalars, *first, mine, got)


def turn_kernel(s_ref, up_own, up_oth, out):
    for i, up in enumerate((up_own, up_oth)):
        turned = up[...].T.reshape(8, 4, 16, TOK)
        for to in range(4):
            out[to, :, i * TOK : (i + 1) * TOK] = turned[:, to].reshape(TOK, TOK)


def turn(scalars, up_own, up_oth):
    quarter = pl.BlockSpec((TOK, 512), lambda b, s: (0, b))
    return call(
        turn_kernel, "turn", (4,), [quarter] * 2, pl.BlockSpec((4, TOK, CHIP), lambda b, s: (0, 0, b)),
        bf(4, TOK, HALF), 0, 2 << 20,
    )(scalars, up_own, up_oth)


def project_kernel(s_ref, up_own, up_oth, w0, w1, w3, wa, wb, out):
    x, yh = s_ref[2], s_ref[3]
    lefts, rights = [], []
    for dx, pair in ((0, (w0[:256], w0[256:])), (1, (w1[:256], w1[256:])), (3, (w3[:256], w3[256:])), (2, (wa, wb))):
        for dy, right in enumerate(pair):
            block = ((x + dx) & 3) * 2 + ((yh + dy) & 1)
            cols = pl.ds(pl.multiple_of(block * 256, 256), 256)
            lefts.append(jnp.concatenate([up_own[:, cols], up_oth[:, cols]], axis=0))
            rights.append(right[...])
    out[...] = dot(jnp.concatenate(lefts, axis=1), jnp.concatenate(rights, axis=0), 1, 0).astype(BF)


def project(scalars, up_own, up_oth, *ws):
    tile = 256
    cols = lambda rows: pl.BlockSpec((rows, tile), lambda n, s: (0, n))
    return call(
        project_kernel, "project", (HALF // tile,),
        [whole(TOK, D), whole(TOK, D), cols(512), cols(512), cols(512), cols(256), cols(256)],
        cols(CHIP), bf(CHIP, HALF), 2 * CHIP * D * HALF, 2 * D * HALF + 3 * CHIP * D,
    )(scalars, up_own, up_oth, *ws)


def scores(s_ref, q, k0, k1, k2):
    core, chip = s_ref[0], s_ref[1]
    key_at = (lax.broadcasted_iota(jnp.int32, (CHIP, CHIP), 0) + core * TOK) & (CHIP - 1)
    query_at = (lax.broadcasted_iota(jnp.int32, (CHIP, CHIP), 1) + core * TOK) & (CHIP - 1)
    near = key_at <= query_at
    shown = jnp.logical_or(near, chip >= 2)
    sm = jnp.where(near, dot(k0, q, 1, 1), dot(k2, q, 1, 1)) * INV_ROOT
    sm = jnp.where(shown, sm, NEGATIVE)
    s1 = jnp.where(chip >= 1, dot(k1, q, 1, 1) * INV_ROOT, NEGATIVE)
    return near, sm, s1


def split(near, pm):
    return jnp.where(near, pm, 0.0).astype(BF), jnp.where(near, 0.0, pm).astype(BF)


def forward_kernel(s_ref, wa_ref, wb_ref, q_r, k0_r, v0_r, k1_r, v1_r, k2_r, v2_r, up_t, out_r, log_r):
    out_r[:, CHIP:] = up_t[...]
    for i in range(TOGETHER):
        h = slice(i * HD, (i + 1) * HD)
        near, sm, s1 = scores(s_ref, q_r[:, h], k0_r[:, h], k1_r[:, h], k2_r[:, h])
        top = jnp.maximum(jnp.max(sm, axis=0, keepdims=True), jnp.max(s1, axis=0, keepdims=True))
        em = jnp.exp(sm - top)
        e1 = jnp.exp(s1 - top)
        total = jnp.sum(em, axis=0, keepdims=True) + jnp.sum(e1, axis=0, keepdims=True)
        log_r[i] = top + jnp.log(total)
        scale = 1.0 / total
        p0, p2 = split(near, em * scale)
        p1 = (e1 * scale).astype(BF)
        att = dot(v0_r[:, h].T, p0, 1, 0) + dot(v1_r[:, h].T, p1, 1, 0) + dot(v2_r[:, h].T, p2, 1, 0)
        att = att.astype(BF).T
        for to in range(4):
            out_r[to, :CHIP, h] = att


def at(first):
    return pl.BlockSpec((CHIP, WIDE), lambda h, s: (0, first * STEPS + h))


def deep(n, rows):
    return pl.BlockSpec((n, rows, WIDE), lambda h, s: (0, 0, h))


LOGS = pl.BlockSpec((TOGETHER, 1, CHIP), lambda h, s: (h, 0, 0))


def forward(scalars, wa, wb, after, own, before, up_t):
    return call(
        forward_kernel, "forward", (STEPS,), [AFTER, AFTER, at(0), at(1), at(2), at(1), at(2), at(1), at(2), deep(4, TOK)],
        [deep(4, CHIP + TOK), LOGS], [bf(4, CHIP + TOK, HALF), jax.ShapeDtypeStruct((HEADS, 1, CHIP), F32)],
        2 * 6 * CHIP * CHIP * HD * HEADS, 6 << 20, 2 * CHIP * CHIP * HEADS,
    )(scalars, wa, wb, after, after, after, own, own, before, before, up_t)


def backward_kernel(
    s_ref, q_r, k0_r, v0_r, k1_r, v1_r, k2_r, v2_r, do_r, att_r, log_r,
    on_same, on_cross, own_same, own_cross, back_same, back_cross,
):
    for i in range(TOGETHER):
        h = slice(i * HD, (i + 1) * HD)
        q, do = q_r[:, h], do_r[:, h]
        k0, k1, k2 = k0_r[:, h], k1_r[:, h], k2_r[:, h]
        near, sm, s1 = scores(s_ref, q, k0, k1, k2)
        pm = jnp.exp(sm - log_r[i])
        p1 = jnp.exp(s1 - log_r[i])
        p0_low, p2_low = split(near, pm)
        p1_low = p1.astype(BF)
        center = jnp.sum((do.astype(F32) * att_r[0, :, h].astype(F32)).T, axis=0, keepdims=True)
        dm = pm * (jnp.where(near, dot(v0_r[:, h], do, 1, 1), dot(v2_r[:, h], do, 1, 1)) - center)
        d1 = (p1 * (dot(v1_r[:, h], do, 1, 1) - center)).astype(BF)
        d0, d2 = split(near, dm)
        dq = dot(k0.T, d0, 1, 0) + dot(k1.T, d1, 1, 0) + dot(k2.T, d2, 1, 0)
        dq = (dq * INV_ROOT).astype(BF).T
        on_same[0, :, h], on_cross[0, :, h] = dq[:TOK], dq[TOK:]
        for same, cross, n, d, p in (
            (on_same, on_cross, 1, d0, p0_low), (own_same, own_cross, 0, d1, p1_low), (back_same, back_cross, 0, d2, p2_low)
        ):
            dk = (dot(d, q, 1, 0) * INV_ROOT).astype(BF)
            dv = dot(p, do, 1, 0).astype(BF)
            same[n, :, h], cross[n, :, h] = dk[:TOK], dk[TOK:]
            same[n + 1, :, h], cross[n + 1, :, h] = dv[:TOK], dv[TOK:]


def backward(scalars, after, own, before, do, att, log):
    return call(
        backward_kernel, "backward", (STEPS,),
        [at(0), at(1), at(2), at(1), at(2), at(1), at(2), at(0), deep(1, CHIP), LOGS],
        [deep(n, TOK) for n in (3, 3, 2, 2, 2, 2)], [bf(n, TOK, HALF) for n in (3, 3, 2, 2, 2, 2)],
        2 * 15 * CHIP * CHIP * HD * HEADS, 12 << 20, 2 * CHIP * CHIP * HEADS,
    )(scalars, after, after, after, own, own, before, before, do, att, log)


def weight_kernel(s_ref, on_ref, own_ref, back_ref, up_t, att, out):
    width = att.shape[2]
    rows = [[up_t[i, CHIP:, b * CHIP : (b + 1) * CHIP] for i in range(4)] for b in range(4)]
    left = jnp.concatenate([jnp.concatenate(row, axis=1) for row in rows], axis=0)
    total = dot(left, att[...].reshape(4 * CHIP, width), 1, 0)
    total = total.reshape(32, 2, 8, width)
    for half in range(2):
        out[half] = total[:, half].reshape(256, width).astype(BF)


def weight_partial(scalars, got, *sent):
    tile = 512
    return call(
        weight_kernel, "weight_partial", (HALF // tile,),
        [AFTER] * 3 + [whole(4, CHIP + TOK, HALF), pl.BlockSpec((4, CHIP, tile), lambda n, s: (0, 0, n))],
        pl.BlockSpec((2, 256, tile), lambda n, s: (0, 0, n)), bf(2, 256, HALF),
        2 * CHIP * D * HALF, 4 << 20,
    )(scalars, *sent, got, got)


def plus(*terms):
    total = terms[0].astype(F32)
    for t in terms[1:]:
        total = total + t.astype(F32)
    return total


def finish_kernel(s_ref, part_ref, on_s, on_x, own_s, own_x, back_s, back_x, grad_q, grad_kv):
    for first, on, own, back in ((s_ref[0], on_s, own_s, back_s), (1 - s_ref[0], on_x, own_x, back_x)):
        cols = pl.ds(pl.multiple_of(first * HALF, HALF), HALF)
        grad_q[:, cols] = on[0]
        for i in range(2):
            grad_kv[i, :, cols] = plus(on[1 + i], own[i], back[i]).astype(BF)


def finish(scalars, part, *terms):
    return call(
        finish_kernel, "finish", (1,), [AFTER] + [whole(n, TOK, HALF) for n in (3, 3, 2, 2, 2, 2)],
        [whole(TOK, D), whole(2, TOK, D)], [bf(TOK, D), bf(2, TOK, D)], 0, 5 << 20,
    )(scalars, part, *terms)


def add_kernel(s_ref, on_ref, back_ref, parts, out):
    out[...] = plus(*[parts[i] for i in range(4)]).astype(BF)


def sum_over_y(scalars, part, *sent):
    parts = lax.all_to_all(part.reshape(4, 128, HALF), ("yh", "yl"), 0, 0, tiled=True)
    return call(
        add_kernel, "add_y", (1,), [AFTER] * 2 + [whole(4, 128, HALF)], whole(128, HALF), bf(128, HALF), 0, 2 << 20
    )(scalars, *sent, parts)


def sum_over_z(part):
    mine = lax.all_to_all(part.reshape(16, 8, HALF), ("z", "core"), 0, 0, tiled=True)
    mine = jnp.sum(mine.reshape(8, 2, 8, HALF).astype(F32), axis=0)
    return jnp.concatenate([mine[0], mine[1]], axis=1)


def shards(queries, keys_values, upstream, out_weight):
    core = lax.axis_index("core")
    x, yh = lax.axis_index("x"), lax.axis_index("yh")
    chip = (lax.axis_index("yl") * 8 + lax.axis_index("z") + 1) & 15
    scalars = jnp.stack([core, chip, x, yh]).astype(jnp.int32)

    w = lax.dynamic_slice_in_dim(out_weight, core * HALF, HALF, 1)
    up_own = to_chip(upstream[0], -1)
    w0 = pack(scalars, w, to_y_neighbour(w), up_own)
    w3, w1 = to_x(w0, 1), to_x(w0, -1)
    wa, wb = to_x(w3[:256], 1), to_x(w1[256:], -1)
    kv = jnp.swapaxes(keys_values[0], 0, 1)
    mine, theirs = cut(scalars, queries[0], kv)
    mine = pack(scalars, mine, to_core(theirs))
    after, before = to_chip(mine, -1), to_chip(mine, 1)
    up_oth = to_core(up_own)
    up_t = turn(scalars, up_own, up_oth)

    sent, log = forward(scalars, wa, wb, after, mine, before, up_t)
    do = project(scalars, up_own, up_oth, w0, w1, w3, wa, wb)
    on_s, on_x, own_s, own_x, back_s, back_x = backward(scalars, after, mine, before, do, sent, log)
    got = lax.all_to_all(sent, "x", 0, 0, tiled=True)
    on_s, on_x = to_chip(on_s, 1), to_chip(on_x, 1, True)
    back_s, back_x = to_chip(back_s, -1), to_chip(back_x, -1, True)
    own_x = to_core(own_x)
    part = weight_partial(scalars, got, on_s, own_x, back_s)
    part = sum_over_y(scalars, part, on_x, back_x)
    grad_q, grad_kv = finish(scalars, part, on_s, on_x, own_s, own_x, back_s, back_x)
    return grad_q[None], jnp.swapaxes(grad_kv, 0, 1)[None], sum_over_z(part)


def solution(mesh):
    names = tuple(name for name, _ in SPLIT)
    fine = Mesh(mesh.devices.reshape([size for _, size in SPLIT]), names)
    return jax.shard_map(
        shards,
        mesh=fine,
        in_specs=(P(FSDP, CTX, None), P(FSDP, CTX, None, None), P(FSDP, CTX, None), P(FSDP, None)),
        out_specs=(P(FSDP, CTX, None), P(FSDP, CTX, None, None), P(CTX + FSDP, None)),
        check_vma=False,
    )
```

```python
import jax
import jax.numpy as jnp
from jax import lax
from jax.experimental import pallas as pl
from jax.experimental.pallas import tpu as pltpu
from jax.sharding import Mesh
from jax.sharding import PartitionSpec as P

SPLIT = (("yl", 2), ("z", 8), ("core", 2), ("x", 4), ("yh", 2))
CTX = ("yl", "z", "core")
FSDP = ("x", "yh")

TOK = 128
CHIP = 256
HEADS = 8
HD = 128
HALF = HEADS * HD
D = 2048
TOGETHER = 2
STEPS = HEADS // TOGETHER
WIDE = TOGETHER * HD
NEGATIVE = -1e30
INV_ROOT = HD**-0.5
BF = jnp.bfloat16
F32 = jnp.float32
VMEM = {"cut": 56, "project": 56, "forward": 56, "backward": 56, "weight_partial": 56, "finish": 56, "merge": 8, "meet": 8, "pack": 8, "turn": 8, "add_y": 8}


def dot(a, b, ca, cb):
    return lax.dot_general(a, b, (((ca,), (cb,)), ((), ())), preferred_element_type=F32)


def to_chip(a, by, cross=False):
    pairs = []
    for i in range(16):
        for core in range(2):
            pairs.append((2 * i + core, (i + by) % 16 * 2 + (1 - core if cross else core)))
    return lax.ppermute(a, CTX, pairs)


def to_core(a):
    return lax.ppermute(a, "core", [(0, 1), (1, 0)])


def to_x(a, by):
    return lax.ppermute(a, "x", [(i, (i + by) % 4) for i in range(4)])


def to_y_neighbour(a):
    return lax.ppermute(a, ("yl", "yh"), [(0, 3), (3, 0), (1, 2), (2, 1)])


def call(body, name, grid, in_specs, out_specs, out_shape, flops, moved, exps=0):
    return pl.pallas_call(
        body,
        grid_spec=pltpu.PrefetchScalarGridSpec(
            num_scalar_prefetch=1, grid=grid, in_specs=in_specs, out_specs=out_specs
        ),
        out_shape=out_shape,
        compiler_params=pltpu.CompilerParams(vmem_limit_bytes=VMEM[name] << 20),
        cost_estimate=pl.CostEstimate(flops=flops, bytes_accessed=moved, transcendentals=exps),
        name=name,
    )


AFTER = pl.BlockSpec(memory_space=pl.ANY)


def whole(*shape):
    return pl.BlockSpec(shape, lambda *_: (0,) * len(shape))


def bf(*shape):
    return jax.ShapeDtypeStruct(shape, BF)


def cut_kernel(s_ref, q, kv, mine, theirs):
    own = s_ref[0] * HALF
    for first, out in ((own, mine), (HALF - own, theirs)):
        at = pl.ds(pl.multiple_of(first, HALF), HALF)
        out[:, :HALF] = q[:, at]
        out[:, HALF : 2 * HALF] = kv[0, :, at]
        out[:, 2 * HALF :] = kv[1, :, at]


def cut(scalars, q, kv):
    return call(
        cut_kernel, "cut", (1,), [whole(TOK, D), whole(2, TOK, D)], [whole(TOK, 3 * HALF)] * 2,
        [bf(TOK, 3 * HALF)] * 2, 0, 4 << 20,
    )(scalars, q, kv)


def pack_kernel(s_ref, *refs):
    mine, got, out = refs[-3:]
    rows = mine.shape[0]
    out[:rows] = mine[...]
    out[rows:] = got[...]


def pack(scalars, mine, got, *first):
    rows, width = mine.shape
    part = lambda n: pl.BlockSpec((n, HALF), lambda i, s: (0, i))
    return call(
        pack_kernel, "pack", (width // HALF,), [AFTER] * len(first) + [part(rows)] * 2, part(2 * rows),
        bf(2 * rows, width), 0, 8 * rows * width,
    )(scalars, *first, mine, got)


def meet_kernel(s_ref, w, got, up, w_out, up_out):
    w_out[:256], w_out[256:] = w[...], got[...]
    up_out[...] = up[...]


def meet(scalars, w, got, up):
    return call(
        meet_kernel, "meet", (1,), [whole(256, HALF)] * 2 + [whole(TOK, D)], [whole(512, HALF), whole(TOK, D)],
        [bf(512, HALF), bf(TOK, D)], 0, 3 << 20,
    )(scalars, w, got, up)


def turn_kernel(s_ref, up_own, up_oth, out):
    for i, up in enumerate((up_own, up_oth)):
        turned = up[...].T.reshape(8, 4, 16, TOK)
        for to in range(4):
            out[to, :, i * TOK : (i + 1) * TOK] = turned[:, to].reshape(TOK, TOK)


def turn(scalars, up_own, up_oth):
    quarter = pl.BlockSpec((TOK, 512), lambda b, s: (0, b))
    return call(
        turn_kernel, "turn", (4,), [quarter] * 2, pl.BlockSpec((4, TOK, CHIP), lambda b, s: (0, 0, b)),
        bf(4, TOK, HALF), 0, 2 << 20,
    )(scalars, up_own, up_oth)


def project_kernel(s_ref, up_own, up_oth, w0, w1, w3, wa, wb, out):
    x, yh = s_ref[2], s_ref[3]
    lefts, rights = [], []
    for dx, pair in ((0, (w0[:256], w0[256:])), (1, (w1[:256], w1[256:])), (3, (w3[:256], w3[256:])), (2, (wa, wb))):
        for dy, right in enumerate(pair):
            block = ((x + dx) & 3) * 2 + ((yh + dy) & 1)
            cols = pl.ds(pl.multiple_of(block * 256, 256), 256)
            lefts.append(jnp.concatenate([up_own[:, cols], up_oth[:, cols]], axis=0))
            rights.append(right[...])
    out[...] = dot(jnp.concatenate(lefts, axis=1), jnp.concatenate(rights, axis=0), 1, 0).astype(BF)


def project(scalars, up_own, up_oth, *ws):
    tile = 512
    cols = lambda rows: pl.BlockSpec((rows, tile), lambda n, s: (0, n))
    return call(
        project_kernel, "project", (HALF // tile,),
        [whole(TOK, D), whole(TOK, D), cols(512), cols(512), cols(512), cols(256), cols(256)],
        cols(CHIP), bf(CHIP, HALF), 2 * CHIP * D * HALF, 2 * D * HALF + 3 * CHIP * D,
    )(scalars, up_own, up_oth, *ws)


def scores(s_ref, q, k0, k1, k2):
    core, chip = s_ref[0], s_ref[1]
    key_at = (lax.broadcasted_iota(jnp.int32, (CHIP, CHIP), 0) + core * TOK) & (CHIP - 1)
    query_at = (lax.broadcasted_iota(jnp.int32, (CHIP, CHIP), 1) + core * TOK) & (CHIP - 1)
    near = key_at <= query_at
    shown = jnp.logical_or(near, chip >= 2)
    sm = jnp.where(near, dot(k0, q, 1, 1), dot(k2, q, 1, 1)) * INV_ROOT
    sm = jnp.where(shown, sm, NEGATIVE)
    s1 = jnp.where(chip >= 1, dot(k1, q, 1, 1) * INV_ROOT, NEGATIVE)
    return near, sm, s1


def split(near, pm):
    return jnp.where(near, pm, 0.0).astype(BF), jnp.where(near, 0.0, pm).astype(BF)


def forward_kernel(s_ref, wa_ref, wb_ref, q_r, k0_r, v0_r, k1_r, v1_r, k2_r, v2_r, up_t, out_r, log_r):
    out_r[:, CHIP:] = up_t[...]
    for i in range(TOGETHER):
        h = slice(i * HD, (i + 1) * HD)
        near, sm, s1 = scores(s_ref, q_r[:, h], k0_r[:, h], k1_r[:, h], k2_r[:, h])
        top = jnp.maximum(jnp.max(sm, axis=0, keepdims=True), jnp.max(s1, axis=0, keepdims=True))
        em = jnp.exp(sm - top)
        e1 = jnp.exp(s1 - top)
        total = jnp.sum(em, axis=0, keepdims=True) + jnp.sum(e1, axis=0, keepdims=True)
        log_r[i] = top + jnp.log(total)
        scale = 1.0 / total
        p0, p2 = split(near, em * scale)
        p1 = (e1 * scale).astype(BF)
        att = dot(v0_r[:, h].T, p0, 1, 0) + dot(v1_r[:, h].T, p1, 1, 0) + dot(v2_r[:, h].T, p2, 1, 0)
        att = att.astype(BF).T
        for to in range(4):
            out_r[to, :CHIP, h] = att


def at(first):
    return pl.BlockSpec((CHIP, WIDE), lambda h, s: (0, first * STEPS + h))


def deep(n, rows):
    return pl.BlockSpec((n, rows, WIDE), lambda h, s: (0, 0, h))


LOGS = pl.BlockSpec((TOGETHER, 1, CHIP), lambda h, s: (h, 0, 0))


def forward(scalars, wa, wb, after, own, before, up_t):
    return call(
        forward_kernel, "forward", (STEPS,), [AFTER, AFTER, at(0), at(1), at(2), at(1), at(2), at(1), at(2), deep(4, TOK)],
        [deep(4, CHIP + TOK), LOGS], [bf(4, CHIP + TOK, HALF), jax.ShapeDtypeStruct((HEADS, 1, CHIP), F32)],
        2 * 6 * CHIP * CHIP * HD * HEADS, 6 << 20, 2 * CHIP * CHIP * HEADS,
    )(scalars, wa, wb, after, after, after, own, own, before, before, up_t)


def backward_kernel(
    s_ref, q_r, k0_r, v0_r, k1_r, v1_r, k2_r, v2_r, do_r, att_r, log_r,
    on_same, on_cross, own_r, back_r,
):
    for i in range(TOGETHER):
        h = slice(i * HD, (i + 1) * HD)
        q, do = q_r[:, h], do_r[:, h]
        k0, k1, k2 = k0_r[:, h], k1_r[:, h], k2_r[:, h]
        near, sm, s1 = scores(s_ref, q, k0, k1, k2)
        pm = jnp.exp(sm - log_r[i])
        p1 = jnp.exp(s1 - log_r[i])
        p0_low, p2_low = split(near, pm)
        p1_low = p1.astype(BF)
        center = jnp.sum((do.astype(F32) * att_r[0, :, h].astype(F32)).T, axis=0, keepdims=True)
        dm = pm * (jnp.where(near, dot(v0_r[:, h], do, 1, 1), dot(v2_r[:, h], do, 1, 1)) - center)
        d1 = (p1 * (dot(v1_r[:, h], do, 1, 1) - center)).astype(BF)
        d0, d2 = split(near, dm)
        dq = dot(k0.T, d0, 1, 0) + dot(k1.T, d1, 1, 0) + dot(k2.T, d2, 1, 0)
        dq = (dq * INV_ROOT).astype(BF).T
        on_same[0, :, h], on_cross[0, :, h] = dq[:TOK], dq[TOK:]
        for n, d, p in ((1, d0, p0_low), (2, d1, p1_low), (3, d2, p2_low)):
            dk = (dot(d, q, 1, 0) * INV_ROOT).astype(BF)
            dv = dot(p, do, 1, 0).astype(BF)
            if n == 1:
                on_same[1, :, h], on_cross[1, :, h] = dk[:TOK], dk[TOK:]
                on_same[2, :, h], on_cross[2, :, h] = dv[:TOK], dv[TOK:]
            else:
                out = own_r if n == 2 else back_r
                out[0, :, h], out[1, :, h] = dk, dv


def backward(scalars, after, own, before, do, att, log):
    return call(
        backward_kernel, "backward", (STEPS,),
        [at(0), at(1), at(2), at(1), at(2), at(1), at(2), at(0), deep(1, CHIP), LOGS],
        [deep(3, TOK)] * 2 + [deep(2, CHIP)] * 2, [bf(3, TOK, HALF)] * 2 + [bf(2, CHIP, HALF)] * 2,
        2 * 15 * CHIP * CHIP * HD * HEADS, 12 << 20, 2 * CHIP * CHIP * HEADS,
    )(scalars, after, after, after, own, own, before, before, do, att, log)


def weight_kernel(s_ref, on_ref, up_t, att, out):
    width = att.shape[2]
    rows = [[up_t[i, CHIP:, b * CHIP : (b + 1) * CHIP] for i in range(4)] for b in range(4)]
    left = jnp.concatenate([jnp.concatenate(row, axis=1) for row in rows], axis=0)
    total = dot(left, att[...].reshape(4 * CHIP, width), 1, 0)
    total = total.reshape(32, 2, 8, width)
    for half in range(2):
        out[half] = total[:, half].reshape(256, width).astype(BF)


def weight_partial(scalars, got, *sent):
    tile = 512
    return call(
        weight_kernel, "weight_partial", (HALF // tile,),
        [AFTER, whole(4, CHIP + TOK, HALF), pl.BlockSpec((4, CHIP, tile), lambda n, s: (0, 0, n))],
        pl.BlockSpec((2, 256, tile), lambda n, s: (0, 0, n)), bf(2, 256, HALF),
        2 * CHIP * D * HALF, 4 << 20,
    )(scalars, *sent, got, got)


def plus(*terms):
    total = terms[0].astype(F32)
    for t in terms[1:]:
        total = total + t.astype(F32)
    return total


def merge_kernel(s_ref, own, back, mine, theirs):
    for i in range(2):
        total = plus(own[i], back[i]).astype(BF)
        mine[i], theirs[i] = total[:TOK], total[TOK:]


def merge(scalars, own, back):
    tile = 512
    part = lambda rows: pl.BlockSpec((2, rows, tile), lambda i, s: (0, 0, i))
    return call(
        merge_kernel, "merge", (HALF // tile,), [part(CHIP)] * 2, [part(TOK)] * 2, [bf(2, TOK, HALF)] * 2, 0, 3 << 20
    )(scalars, own, back)


def finish_kernel(s_ref, part_ref, on_s, on_x, rest_s, rest_x, grad_q, grad_kv):
    for first, on, rest in ((s_ref[0], on_s, rest_s), (1 - s_ref[0], on_x, rest_x)):
        cols = pl.ds(pl.multiple_of(first * HALF, HALF), HALF)
        grad_q[:, cols] = on[0]
        for i in range(2):
            grad_kv[i, :, cols] = plus(on[1 + i], rest[i]).astype(BF)


def finish(scalars, part, *terms):
    return call(
        finish_kernel, "finish", (1,), [AFTER] + [whole(n, TOK, HALF) for n in (3, 3, 2, 2)],
        [whole(TOK, D), whole(2, TOK, D)], [bf(TOK, D), bf(2, TOK, D)], 0, 5 << 20,
    )(scalars, part, *terms)


def add_kernel(s_ref, on_ref, back_ref, parts, out):
    out[...] = plus(*[parts[i] for i in range(4)]).astype(BF)


def sum_over_y(scalars, part, *sent):
    parts = lax.all_to_all(part.reshape(4, 128, HALF), ("yh", "yl"), 0, 0, tiled=True)
    return call(
        add_kernel, "add_y", (1,), [AFTER] * 2 + [whole(4, 128, HALF)], whole(128, HALF), bf(128, HALF), 0, 2 << 20
    )(scalars, *sent, parts)


def sum_over_z(part):
    mine = lax.all_to_all(part.reshape(16, 8, HALF), ("z", "core"), 0, 0, tiled=True)
    mine = jnp.sum(mine.reshape(8, 2, 8, HALF).astype(F32), axis=0)
    return jnp.concatenate([mine[0], mine[1]], axis=1)


def shards(queries, keys_values, upstream, out_weight):
    core = lax.axis_index("core")
    x, yh = lax.axis_index("x"), lax.axis_index("yh")
    chip = (lax.axis_index("yl") * 8 + lax.axis_index("z") + 1) & 15
    scalars = jnp.stack([core, chip, x, yh]).astype(jnp.int32)

    w = lax.dynamic_slice_in_dim(out_weight, core * HALF, HALF, 1)
    w0, up_own = meet(scalars, w, to_y_neighbour(w), to_chip(upstream[0], -1))
    kv = jnp.swapaxes(keys_values[0], 0, 1)
    mine, theirs = cut(scalars, queries[0], kv)
    up_oth = to_core(up_own)
    mine = pack(scalars, mine, to_core(theirs), up_oth)
    after, before = to_chip(mine, -1), to_chip(mine, 1)
    w3, w1 = to_x(w0, 1), to_x(w0, -1)
    wa, wb = to_x(w3[:256], 1), to_x(w1[256:], -1)
    up_t = turn(scalars, up_own, up_oth)

    sent, log = forward(scalars, wa, wb, after, mine, before, up_t)
    do = project(scalars, up_own, up_oth, w0, w1, w3, wa, wb)
    on_s, on_x, own, back = backward(scalars, after, mine, before, do, sent, log)
    got = lax.all_to_all(sent, "x", 0, 0, tiled=True)
    on_s, on_x = to_chip(on_s, 1), to_chip(on_x, 1, True)
    rest_s, rest_x = merge(scalars, own, to_chip(back, -1))
    rest_x = to_core(rest_x)
    part = sum_over_y(scalars, weight_partial(scalars, got, on_s), on_x, rest_x)
    grad_q, grad_kv = finish(scalars, part, on_s, on_x, rest_s, rest_x)
    return grad_q[None], jnp.swapaxes(grad_kv, 0, 1)[None], sum_over_z(part)


def solution(mesh):
    names = tuple(name for name, _ in SPLIT)
    fine = Mesh(mesh.devices.reshape([size for _, size in SPLIT]), names)
    return jax.shard_map(
        shards,
        mesh=fine,
        in_specs=(P(FSDP, CTX, None), P(FSDP, CTX, None, None), P(FSDP, CTX, None), P(FSDP, None)),
        out_specs=(P(FSDP, CTX, None), P(FSDP, CTX, None, None), P(CTX + FSDP, None)),
        check_vma=False,
    )
```

```python
import jax
import jax.numpy as jnp
from jax import lax
from jax.experimental import pallas as pl
from jax.experimental.pallas import tpu as pltpu
from jax.sharding import Mesh
from jax.sharding import PartitionSpec as P

SPLIT = (("yl", 2), ("z", 8), ("core", 2), ("x", 4), ("yh", 2))
CTX = ("yl", "z", "core")
FSDP = ("x", "yh")

TOK = 128
CHIP = 256
HEADS = 8
HD = 128
HALF = HEADS * HD
D = 2048
TOGETHER = 2
STEPS = HEADS // TOGETHER
WIDE = TOGETHER * HD
NEGATIVE = -1e30
INV_ROOT = HD**-0.5
BF = jnp.bfloat16
F32 = jnp.float32
VMEM = {"cut": 56, "forward": 56, "backward": 56, "weight_partial": 56, "finish": 56, "merge": 8, "pair": 8, "meet": 8, "pack": 8, "turn": 8, "add_y": 8}


def dot(a, b, ca, cb):
    return lax.dot_general(a, b, (((ca,), (cb,)), ((), ())), preferred_element_type=F32)


def to_chip(a, by, cross=False):
    pairs = []
    for i in range(16):
        for core in range(2):
            pairs.append((2 * i + core, (i + by) % 16 * 2 + (1 - core if cross else core)))
    return lax.ppermute(a, CTX, pairs)


def to_core(a):
    return lax.ppermute(a, "core", [(0, 1), (1, 0)])


def to_x(a, by):
    return lax.ppermute(a, "x", [(i, (i + by) % 4) for i in range(4)])


def to_y_neighbour(a):
    return lax.ppermute(a, ("yl", "yh"), [(0, 3), (3, 0), (1, 2), (2, 1)])


def to_y_other(a):
    return lax.ppermute(a, "yl", [(0, 1), (1, 0)])


def call(body, name, grid, in_specs, out_specs, out_shape, flops, moved, exps=0):
    return pl.pallas_call(
        body,
        grid_spec=pltpu.PrefetchScalarGridSpec(
            num_scalar_prefetch=1, grid=grid, in_specs=in_specs, out_specs=out_specs
        ),
        out_shape=out_shape,
        compiler_params=pltpu.CompilerParams(vmem_limit_bytes=VMEM[name] << 20),
        cost_estimate=pl.CostEstimate(flops=flops, bytes_accessed=moved, transcendentals=exps),
        name=name,
    )


AFTER = pl.BlockSpec(memory_space=pl.ANY)


def whole(*shape):
    return pl.BlockSpec(shape, lambda *_: (0,) * len(shape))


def bf(*shape):
    return jax.ShapeDtypeStruct(shape, BF)


def cut_kernel(s_ref, q, kv, mine, theirs):
    own = s_ref[0] * HALF
    for first, out in ((own, mine), (HALF - own, theirs)):
        at = pl.ds(pl.multiple_of(first, HALF), HALF)
        out[:, :HALF] = q[:, at]
        out[:, HALF : 2 * HALF] = kv[0, :, at]
        out[:, 2 * HALF :] = kv[1, :, at]


def cut(scalars, q, kv):
    return call(
        cut_kernel, "cut", (1,), [whole(TOK, D), whole(2, TOK, D)], [whole(TOK, 3 * HALF)] * 2,
        [bf(TOK, 3 * HALF)] * 2, 0, 4 << 20,
    )(scalars, q, kv)


def pack_kernel(s_ref, *refs):
    mine, got, out = refs[-3:]
    rows = mine.shape[0]
    out[:rows] = mine[...]
    out[rows:] = got[...]


def pack(scalars, mine, got, *first):
    rows, width = mine.shape
    part = lambda n: pl.BlockSpec((n, HALF), lambda i, s: (0, i))
    return call(
        pack_kernel, "pack", (width // HALF,), [AFTER] * len(first) + [part(rows)] * 2, part(2 * rows),
        bf(2 * rows, width), 0, 8 * rows * width,
    )(scalars, *first, mine, got)


def meet_kernel(s_ref, w, got, up, w_out, up_out):
    w_out[:256], w_out[256:] = w[...], got[...]
    up_out[...] = up[...]


def meet(scalars, w, got, up):
    return call(
        meet_kernel, "meet", (1,), [whole(256, HALF)] * 2 + [whole(TOK, D)], [whole(512, HALF), whole(TOK, D)],
        [bf(512, HALF), bf(TOK, D)], 0, 3 << 20,
    )(scalars, w, got, up)


def turn_kernel(s_ref, up_own, up_oth, out):
    for i, up in enumerate((up_own, up_oth)):
        turned = up[...].T.reshape(8, 4, 16, TOK)
        for to in range(4):
            out[to, :, i * TOK : (i + 1) * TOK] = turned[:, to].reshape(TOK, TOK)


def turn(scalars, up_own, up_oth):
    quarter = pl.BlockSpec((TOK, 512), lambda b, s: (0, b))
    return call(
        turn_kernel, "turn", (4,), [quarter] * 2, pl.BlockSpec((4, TOK, CHIP), lambda b, s: (0, 0, b)),
        bf(4, TOK, HALF), 0, 2 << 20,
    )(scalars, up_own, up_oth)


def scores(s_ref, q, k0, k1, k2):
    core, chip = s_ref[0], s_ref[1]
    key_at = (lax.broadcasted_iota(jnp.int32, (CHIP, CHIP), 0) + core * TOK) & (CHIP - 1)
    query_at = (lax.broadcasted_iota(jnp.int32, (CHIP, CHIP), 1) + core * TOK) & (CHIP - 1)
    near = key_at <= query_at
    shown = jnp.logical_or(near, chip >= 2)
    sm = jnp.where(near, dot(k0, q, 1, 1), dot(k2, q, 1, 1)) * INV_ROOT
    sm = jnp.where(shown, sm, NEGATIVE)
    s1 = jnp.where(chip >= 1, dot(k1, q, 1, 1) * INV_ROOT, NEGATIVE)
    return near, sm, s1


def split(near, pm):
    return jnp.where(near, pm, 0.0).astype(BF), jnp.where(near, 0.0, pm).astype(BF)


def forward_kernel(s_ref, wa_ref, wb_ref, q_r, k0_r, v0_r, k1_r, v1_r, k2_r, v2_r, up_t, out_r, log_r):
    out_r[:, CHIP:] = up_t[...]
    for i in range(TOGETHER):
        h = slice(i * HD, (i + 1) * HD)
        near, sm, s1 = scores(s_ref, q_r[:, h], k0_r[:, h], k1_r[:, h], k2_r[:, h])
        top = jnp.maximum(jnp.max(sm, axis=0, keepdims=True), jnp.max(s1, axis=0, keepdims=True))
        em = jnp.exp(sm - top)
        e1 = jnp.exp(s1 - top)
        total = jnp.sum(em, axis=0, keepdims=True) + jnp.sum(e1, axis=0, keepdims=True)
        log_r[i] = top + jnp.log(total)
        scale = 1.0 / total
        p0, p2 = split(near, em * scale)
        p1 = (e1 * scale).astype(BF)
        att = dot(v0_r[:, h].T, p0, 1, 0) + dot(v1_r[:, h].T, p1, 1, 0) + dot(v2_r[:, h].T, p2, 1, 0)
        att = att.astype(BF).T
        for to in range(4):
            out_r[to, :CHIP, h] = att


def at(first):
    return pl.BlockSpec((CHIP, WIDE), lambda h, s: (0, first * STEPS + h))


def deep(n, rows):
    return pl.BlockSpec((n, rows, WIDE), lambda h, s: (0, 0, h))


LOGS = pl.BlockSpec((TOGETHER, 1, CHIP), lambda h, s: (h, 0, 0))


def forward(scalars, wa, wb, after, own, before, up_t):
    return call(
        forward_kernel, "forward", (STEPS,), [AFTER, AFTER, at(0), at(1), at(2), at(1), at(2), at(1), at(2), deep(4, TOK)],
        [deep(4, CHIP + TOK), LOGS], [bf(4, CHIP + TOK, HALF), jax.ShapeDtypeStruct((HEADS, 1, CHIP), F32)],
        2 * 6 * CHIP * CHIP * HD * HEADS, 6 << 20, 2 * CHIP * CHIP * HEADS,
    )(scalars, wa, wb, after, after, after, own, own, before, before, up_t)


def backward_kernel(
    s_ref, q_r, k0_r, v0_r, k1_r, v1_r, k2_r, v2_r, att_r, log_r, up_own, up_oth, w0, w1, w3, wa, wb,
    on_same, on_cross, own_r, back_r, up,
):
    x, yh = s_ref[2], s_ref[3]

    @pl.when(pl.program_id(0) == 0)
    def _():
        for n, (dx, dy) in enumerate(((0, 0), (0, 1), (1, 0), (1, 1), (3, 0), (3, 1), (2, 0), (2, 1))):
            block = ((x + dx) & 3) * 2 + ((yh + dy) & 1)
            cols = pl.ds(pl.multiple_of(block * 256, 256), 256)
            up[:TOK, n * 256 : (n + 1) * 256] = up_own[:, cols]
            up[TOK:, n * 256 : (n + 1) * 256] = up_oth[:, cols]

    w = jnp.concatenate([w0[...], w1[...], w3[...], wa[...], wb[...]], axis=0)
    grads = dot(up[...], w, 1, 0).astype(BF)
    for i in range(TOGETHER):
        h = slice(i * HD, (i + 1) * HD)
        q, do = q_r[:, h], grads[:, h]
        k0, k1, k2 = k0_r[:, h], k1_r[:, h], k2_r[:, h]
        near, sm, s1 = scores(s_ref, q, k0, k1, k2)
        pm = jnp.exp(sm - log_r[i])
        p1 = jnp.exp(s1 - log_r[i])
        p0_low, p2_low = split(near, pm)
        p1_low = p1.astype(BF)
        center = jnp.sum((do.astype(F32) * att_r[0, :, h].astype(F32)).T, axis=0, keepdims=True)
        dm = pm * (jnp.where(near, dot(v0_r[:, h], do, 1, 1), dot(v2_r[:, h], do, 1, 1)) - center)
        d1 = (p1 * (dot(v1_r[:, h], do, 1, 1) - center)).astype(BF)
        d0, d2 = split(near, dm)
        dq = dot(k0.T, d0, 1, 0) + dot(k1.T, d1, 1, 0) + dot(k2.T, d2, 1, 0)
        dq = (dq * INV_ROOT).astype(BF).T
        on_same[0, :, h], on_cross[0, :, h] = dq[:TOK], dq[TOK:]
        for n, d, p in ((1, d0, p0_low), (2, d1, p1_low), (3, d2, p2_low)):
            dk = (dot(d, q, 1, 0) * INV_ROOT).astype(BF)
            dv = dot(p, do, 1, 0).astype(BF)
            if n == 1:
                on_same[1, :, h], on_cross[1, :, h] = dk[:TOK], dk[TOK:]
                on_same[2, :, h], on_cross[2, :, h] = dv[:TOK], dv[TOK:]
            else:
                out = own_r if n == 2 else back_r
                out[0, :, h], out[1, :, h] = dk, dv


def backward(scalars, after, own, before, att, log, up_own, up_oth, *ws):
    cols = lambda rows: pl.BlockSpec((rows, WIDE), lambda h, s: (0, h))
    return pl.pallas_call(
        backward_kernel,
        grid_spec=pltpu.PrefetchScalarGridSpec(
            num_scalar_prefetch=1,
            grid=(STEPS,),
            in_specs=[at(0), at(1), at(2), at(1), at(2), at(1), at(2), deep(1, CHIP), LOGS, whole(TOK, D), whole(TOK, D)]
            + [cols(512)] * 3 + [cols(256)] * 2,
            out_specs=[deep(3, TOK)] * 2 + [deep(2, CHIP)] * 2,
            scratch_shapes=[pltpu.VMEM((CHIP, D), BF)],
        ),
        out_shape=[bf(3, TOK, HALF)] * 2 + [bf(2, CHIP, HALF)] * 2,
        compiler_params=pltpu.CompilerParams(vmem_limit_bytes=VMEM["backward"] << 20),
        cost_estimate=pl.CostEstimate(
            flops=2 * CHIP * (15 * CHIP * HD * HEADS + D * HALF), bytes_accessed=18 << 20,
            transcendentals=2 * CHIP * CHIP * HEADS,
        ),
        name="backward",
    )(scalars, after, after, after, own, own, before, before, att, log, up_own, up_oth, *ws)


def weight_kernel(s_ref, on_ref, up_t, att, keep, give):
    width = att.shape[2]
    rows = [[up_t[i, CHIP:, b * CHIP : (b + 1) * CHIP] for i in range(4)] for b in range(4)]
    left = jnp.concatenate([jnp.concatenate(row, axis=1) for row in rows], axis=0)
    total = dot(left, att[...].reshape(4 * CHIP, width), 1, 0)
    total = total.reshape(32, 2, 8, width)
    halves = [total[:, half].reshape(256, width) for half in range(2)]
    keep[...] = jnp.where(s_ref[3] == 0, halves[0], halves[1]).astype(BF)
    give[...] = jnp.where(s_ref[3] == 0, halves[1], halves[0]).astype(BF)


def weight_partial(scalars, got, sent):
    tile = 512
    return call(
        weight_kernel, "weight_partial", (HALF // tile,),
        [AFTER, whole(4, CHIP + TOK, HALF), pl.BlockSpec((4, CHIP, tile), lambda n, s: (0, 0, n))],
        [pl.BlockSpec((256, tile), lambda n, s: (0, n))] * 2, [bf(256, HALF)] * 2,
        2 * CHIP * D * HALF, 4 << 20,
    )(scalars, sent, got, got)


def plus(*terms):
    total = terms[0].astype(F32)
    for t in terms[1:]:
        total = total + t.astype(F32)
    return total


def merge_kernel(s_ref, own, back, mine, theirs):
    for i in range(2):
        total = plus(own[i], back[i]).astype(BF)
        mine[i], theirs[i] = total[:TOK], total[TOK:]


def merge(scalars, own, back):
    tile = 512
    part = lambda rows: pl.BlockSpec((2, rows, tile), lambda i, s: (0, 0, i))
    return call(
        merge_kernel, "merge", (HALF // tile,), [part(CHIP)] * 2, [part(TOK)] * 2, [bf(2, TOK, HALF)] * 2, 0, 3 << 20
    )(scalars, own, back)


def finish_kernel(s_ref, on_s, on_x, rest_s, rest_x, grad_q, grad_kv):
    for first, on, rest in ((s_ref[0], on_s, rest_s), (1 - s_ref[0], on_x, rest_x)):
        cols = pl.ds(pl.multiple_of(first * HALF, HALF), HALF)
        grad_q[:, cols] = on[0]
        for i in range(2):
            grad_kv[i, :, cols] = plus(on[1 + i], rest[i]).astype(BF)


def finish(scalars, *terms):
    return call(
        finish_kernel, "finish", (1,), [whole(n, TOK, HALF) for n in (3, 3, 2, 2)],
        [whole(TOK, D), whole(2, TOK, D)], [bf(TOK, D), bf(2, TOK, D)], 0, 5 << 20,
    )(scalars, *terms)


def pair_kernel(s_ref, keep, got, mine, theirs):
    yl = s_ref[4]
    for first, out in ((yl, mine), (1 - yl, theirs)):
        rows = pl.ds(pl.multiple_of(first * 128, 128), 128)
        out[...] = plus(keep[rows, :], got[rows, :]).astype(out.dtype)


def add_kernel(s_ref, grad_ref, mine, got, out):
    out[...] = plus(mine[...], got[...]).astype(BF)


def sum_over_y(scalars, keep, give, grad):
    tile = 512
    cols = lambda rows: pl.BlockSpec((rows, tile), lambda n, s: (0, n))
    mine, theirs = call(
        pair_kernel, "pair", (HALF // tile,), [cols(256)] * 2, [cols(128)] * 2,
        [jax.ShapeDtypeStruct((128, HALF), F32), bf(128, HALF)], 0, 2 << 20,
    )(scalars, keep, to_y_neighbour(give))
    return call(
        add_kernel, "add_y", (HALF // tile,), [AFTER] + [cols(128)] * 2, cols(128), bf(128, HALF), 0, 1 << 20
    )(scalars, grad, mine, to_y_other(theirs))


def sum_over_z(part):
    mine = lax.all_to_all(part.reshape(16, 8, HALF), ("z", "core"), 0, 0, tiled=True)
    mine = jnp.sum(mine.reshape(8, 2, 8, HALF).astype(F32), axis=0)
    return jnp.concatenate([mine[0], mine[1]], axis=1)


def shards(queries, keys_values, upstream, out_weight):
    core = lax.axis_index("core")
    x, yh = lax.axis_index("x"), lax.axis_index("yh")
    chip = (lax.axis_index("yl") * 8 + lax.axis_index("z") + 1) & 15
    scalars = jnp.stack([core, chip, x, yh, lax.axis_index("yl")]).astype(jnp.int32)

    w = lax.dynamic_slice_in_dim(out_weight, core * HALF, HALF, 1)
    w0, up_own = meet(scalars, w, to_y_neighbour(w), to_chip(upstream[0], -1))
    kv = jnp.swapaxes(keys_values[0], 0, 1)
    mine, theirs = cut(scalars, queries[0], kv)
    up_oth = to_core(up_own)
    mine = pack(scalars, mine, to_core(theirs), up_oth)
    after, before = to_chip(mine, -1), to_chip(mine, 1)
    w3, w1 = to_x(w0, 1), to_x(w0, -1)
    wa, wb = to_x(w3[:256], 1), to_x(w1[256:], -1)
    up_t = turn(scalars, up_own, up_oth)

    sent, log = forward(scalars, wa, wb, after, mine, before, up_t)
    got = lax.all_to_all(sent, "x", 0, 0, tiled=True)
    on_s, on_x, own, back = backward(
        scalars, after, mine, before, sent, log, up_own, up_oth, w0, w1, w3, wa, wb
    )
    on_s, on_x = to_chip(on_s, 1), to_chip(on_x, 1, True)
    rest_s, rest_x = merge(scalars, own, to_chip(back, -1))
    rest_x = to_core(rest_x)
    keep, give = weight_partial(scalars, got, on_s)
    grad_q, grad_kv = finish(scalars, on_s, on_x, rest_s, rest_x)
    part = sum_over_y(scalars, keep, give, grad_q)
    return grad_q[None], jnp.swapaxes(grad_kv, 0, 1)[None], sum_over_z(part)


def solution(mesh):
    names = tuple(name for name, _ in SPLIT)
    fine = Mesh(mesh.devices.reshape([size for _, size in SPLIT]), names)
    return jax.shard_map(
        shards,
        mesh=fine,
        in_specs=(P(FSDP, CTX, None), P(FSDP, CTX, None, None), P(FSDP, CTX, None), P(FSDP, None)),
        out_specs=(P(FSDP, CTX, None), P(FSDP, CTX, None, None), P(CTX + FSDP, None)),
        check_vma=False,
    )
```

```python
import jax
import jax.numpy as jnp
from jax import lax
from jax.experimental import pallas as pl
from jax.experimental.pallas import tpu as pltpu
from jax.sharding import Mesh
from jax.sharding import PartitionSpec as P

SPLIT = (("yl", 2), ("z", 8), ("core", 2), ("x", 4), ("yh", 2))
CTX = ("yl", "z", "core")
FSDP = ("x", "yh")

TOK = 128
CHIP = 256
HEADS = 8
HD = 128
HALF = HEADS * HD
D = 2048
TOGETHER = 2
STEPS = HEADS // TOGETHER
WIDE = TOGETHER * HD
NEGATIVE = -1e30
INV_ROOT = HD**-0.5
BF = jnp.bfloat16
F32 = jnp.float32
VMEM = {"cut": 56, "forward": 56, "backward": 56, "weight_partial": 56, "finish": 56, "merge": 8, "pair": 8, "meet": 8, "pack": 8, "turn": 8, "add_y": 8}


def dot(a, b, ca, cb):
    return lax.dot_general(a, b, (((ca,), (cb,)), ((), ())), preferred_element_type=F32)


def to_chip(a, by, cross=False):
    pairs = []
    for i in range(16):
        for core in range(2):
            pairs.append((2 * i + core, (i + by) % 16 * 2 + (1 - core if cross else core)))
    return lax.ppermute(a, CTX, pairs)


def to_core(a):
    return lax.ppermute(a, "core", [(0, 1), (1, 0)])


def to_x(a, by):
    return lax.ppermute(a, "x", [(i, (i + by) % 4) for i in range(4)])


def to_y_neighbour(a):
    return lax.ppermute(a, ("yl", "yh"), [(0, 3), (3, 0), (1, 2), (2, 1)])


def call(body, name, grid, in_specs, out_specs, out_shape, flops, moved, exps=0):
    return pl.pallas_call(
        body,
        grid_spec=pltpu.PrefetchScalarGridSpec(
            num_scalar_prefetch=1, grid=grid, in_specs=in_specs, out_specs=out_specs
        ),
        out_shape=out_shape,
        compiler_params=pltpu.CompilerParams(vmem_limit_bytes=VMEM[name] << 20),
        cost_estimate=pl.CostEstimate(flops=flops, bytes_accessed=moved, transcendentals=exps),
        name=name,
    )


AFTER = pl.BlockSpec(memory_space=pl.ANY)


def whole(*shape):
    return pl.BlockSpec(shape, lambda *_: (0,) * len(shape))


def bf(*shape):
    return jax.ShapeDtypeStruct(shape, BF)


def cut_kernel(s_ref, q, kv, mine, theirs):
    own = s_ref[0] * HALF
    for first, out in ((own, mine), (HALF - own, theirs)):
        at = pl.ds(pl.multiple_of(first, HALF), HALF)
        out[:, :HALF] = q[:, at]
        out[:, HALF : 2 * HALF] = kv[0, :, at]
        out[:, 2 * HALF :] = kv[1, :, at]


def cut(scalars, q, kv):
    return call(
        cut_kernel, "cut", (1,), [whole(TOK, D), whole(2, TOK, D)], [whole(TOK, 3 * HALF)] * 2,
        [bf(TOK, 3 * HALF)] * 2, 0, 4 << 20,
    )(scalars, q, kv)


def pack_kernel(s_ref, *refs):
    mine, got, out = refs[-3:]
    rows = mine.shape[0]
    out[:rows] = mine[...]
    out[rows:] = got[...]


def pack(scalars, mine, got, *first):
    rows, width = mine.shape
    part = lambda n: pl.BlockSpec((n, HALF), lambda i, s: (0, i))
    return call(
        pack_kernel, "pack", (width // HALF,), [AFTER] * len(first) + [part(rows)] * 2, part(2 * rows),
        bf(2 * rows, width), 0, 8 * rows * width,
    )(scalars, *first, mine, got)


def meet_kernel(s_ref, w_y, from_left, from_right, to_right, to_left):
    to_right[:256], to_right[256:] = w_y[...], from_left[:128]
    to_left[:256], to_left[256:] = w_y[...], from_right[128:]


def meet(scalars, w_y, from_left, from_right):
    return call(
        meet_kernel, "meet", (1,), [whole(256, HALF)] * 3, [whole(384, HALF)] * 2, [bf(384, HALF)] * 2, 0, 3 << 20
    )(scalars, w_y, from_left, from_right)


def turn_kernel(s_ref, up_own, up_oth, out):
    for i, up in enumerate((up_own, up_oth)):
        turned = up[...].T.reshape(8, 4, 16, TOK)
        for to in range(4):
            out[to, :, i * TOK : (i + 1) * TOK] = turned[:, to].reshape(TOK, TOK)


def turn(scalars, up_own, up_oth):
    quarter = pl.BlockSpec((TOK, 512), lambda b, s: (0, b))
    return call(
        turn_kernel, "turn", (4,), [quarter] * 2, pl.BlockSpec((4, TOK, CHIP), lambda b, s: (0, 0, b)),
        bf(4, TOK, HALF), 0, 2 << 20,
    )(scalars, up_own, up_oth)


PIECES = (
    (0, 0, 0, 256), (0, 1, 0, 256), (3, 0, 0, 256), (1, 0, 0, 256), (3, 1, 0, 256), (2, 0, 0, 128),
    (1, 1, 0, 256), (2, 0, 128, 128), (2, 1, 0, 128), (2, 1, 128, 128),
)


def scores(s_ref, q, k0, k1, k2):
    core, chip = s_ref[0], s_ref[1]
    key_at = (lax.broadcasted_iota(jnp.int32, (CHIP, CHIP), 0) + core * TOK) & (CHIP - 1)
    query_at = (lax.broadcasted_iota(jnp.int32, (CHIP, CHIP), 1) + core * TOK) & (CHIP - 1)
    near = key_at <= query_at
    shown = jnp.logical_or(near, chip >= 2)
    sm = jnp.where(near, dot(k0, q, 1, 1), dot(k2, q, 1, 1)) * INV_ROOT
    sm = jnp.where(shown, sm, NEGATIVE)
    s1 = jnp.where(chip >= 1, dot(k1, q, 1, 1) * INV_ROOT, NEGATIVE)
    return near, sm, s1


def split(near, pm):
    return jnp.where(near, pm, 0.0).astype(BF), jnp.where(near, 0.0, pm).astype(BF)


def forward_kernel(s_ref, wa_ref, wb_ref, q_r, k0_r, v0_r, k1_r, v1_r, k2_r, v2_r, up_t, out_r, log_r):
    out_r[:, CHIP:] = up_t[...]
    for i in range(TOGETHER):
        h = slice(i * HD, (i + 1) * HD)
        near, sm, s1 = scores(s_ref, q_r[:, h], k0_r[:, h], k1_r[:, h], k2_r[:, h])
        top = jnp.maximum(jnp.max(sm, axis=0, keepdims=True), jnp.max(s1, axis=0, keepdims=True))
        em = jnp.exp(sm - top)
        e1 = jnp.exp(s1 - top)
        total = jnp.sum(em, axis=0, keepdims=True) + jnp.sum(e1, axis=0, keepdims=True)
        log_r[i] = top + jnp.log(total)
        scale = 1.0 / total
        p0, p2 = split(near, em * scale)
        p1 = (e1 * scale).astype(BF)
        att = dot(v0_r[:, h].T, p0, 1, 0) + dot(v1_r[:, h].T, p1, 1, 0) + dot(v2_r[:, h].T, p2, 1, 0)
        att = att.astype(BF).T
        for to in range(4):
            out_r[to, :CHIP, h] = att


def at(first):
    return pl.BlockSpec((CHIP, WIDE), lambda h, s: (0, first * STEPS + h))


def deep(n, rows):
    return pl.BlockSpec((n, rows, WIDE), lambda h, s: (0, 0, h))


LOGS = pl.BlockSpec((TOGETHER, 1, CHIP), lambda h, s: (h, 0, 0))


def forward(scalars, wa, wb, after, own, before, up_t):
    return call(
        forward_kernel, "forward", (STEPS,), [AFTER, AFTER, at(0), at(1), at(2), at(1), at(2), at(1), at(2), deep(4, TOK)],
        [deep(4, CHIP + TOK), LOGS], [bf(4, CHIP + TOK, HALF), jax.ShapeDtypeStruct((HEADS, 1, CHIP), F32)],
        2 * 6 * CHIP * CHIP * HD * HEADS, 6 << 20, 2 * CHIP * CHIP * HEADS,
    )(scalars, wa, wb, after, after, after, own, own, before, before, up_t)


def backward_kernel(
    s_ref, q_r, k0_r, v0_r, k1_r, v1_r, k2_r, v2_r, att_r, log_r, up_own, up_oth, *rest
):
    ws, (on_same, on_cross, own_r, back_r, up) = rest[:8], rest[8:]
    x, yh = s_ref[2], s_ref[3]

    @pl.when(pl.program_id(0) == 0)
    def _():
        start = 0
        for dx, dy, first, size in PIECES:
            block = ((x + dx) & 3) * 2 + ((yh + dy) & 1)
            cols = pl.ds(pl.multiple_of(block * 256 + first, 128), size)
            up[:TOK, start : start + size] = up_own[:, cols]
            up[TOK:, start : start + size] = up_oth[:, cols]
            start += size

    w = jnp.concatenate([r[...] for r in ws], axis=0)
    grads = dot(up[...], w, 1, 0).astype(BF)
    for i in range(TOGETHER):
        h = slice(i * HD, (i + 1) * HD)
        q, do = q_r[:, h], grads[:, h]
        k0, k1, k2 = k0_r[:, h], k1_r[:, h], k2_r[:, h]
        near, sm, s1 = scores(s_ref, q, k0, k1, k2)
        pm = jnp.exp(sm - log_r[i])
        p1 = jnp.exp(s1 - log_r[i])
        p0_low, p2_low = split(near, pm)
        p1_low = p1.astype(BF)
        center = jnp.sum((do.astype(F32) * att_r[0, :, h].astype(F32)).T, axis=0, keepdims=True)
        dm = pm * (jnp.where(near, dot(v0_r[:, h], do, 1, 1), dot(v2_r[:, h], do, 1, 1)) - center)
        d1 = (p1 * (dot(v1_r[:, h], do, 1, 1) - center)).astype(BF)
        d0, d2 = split(near, dm)
        dq = dot(k0.T, d0, 1, 0) + dot(k1.T, d1, 1, 0) + dot(k2.T, d2, 1, 0)
        dq = (dq * INV_ROOT).astype(BF).T
        on_same[0, :, h], on_cross[0, :, h] = dq[:TOK], dq[TOK:]
        for n, d, p in ((1, d0, p0_low), (2, d1, p1_low), (3, d2, p2_low)):
            dk = (dot(d, q, 1, 0) * INV_ROOT).astype(BF)
            dv = dot(p, do, 1, 0).astype(BF)
            if n == 1:
                on_same[1, :, h], on_cross[1, :, h] = dk[:TOK], dk[TOK:]
                on_same[2, :, h], on_cross[2, :, h] = dv[:TOK], dv[TOK:]
            else:
                out = own_r if n == 2 else back_r
                out[0, :, h], out[1, :, h] = dk, dv


def backward(scalars, after, own, before, att, log, up_own, up_oth, *ws):
    cols = lambda rows: pl.BlockSpec((rows, WIDE), lambda h, s: (0, h))
    return pl.pallas_call(
        backward_kernel,
        grid_spec=pltpu.PrefetchScalarGridSpec(
            num_scalar_prefetch=1,
            grid=(STEPS,),
            in_specs=[at(0), at(1), at(2), at(1), at(2), at(1), at(2), deep(1, CHIP), LOGS, whole(TOK, D), whole(TOK, D)]
            + [cols(rows) for rows in (256, 256, 256, 256, 384, 384, 128, 128)],
            out_specs=[deep(3, TOK)] * 2 + [deep(2, CHIP)] * 2,
            scratch_shapes=[pltpu.VMEM((CHIP, D), BF)],
        ),
        out_shape=[bf(3, TOK, HALF)] * 2 + [bf(2, CHIP, HALF)] * 2,
        compiler_params=pltpu.CompilerParams(vmem_limit_bytes=VMEM["backward"] << 20),
        cost_estimate=pl.CostEstimate(
            flops=2 * CHIP * (15 * CHIP * HD * HEADS + D * HALF), bytes_accessed=18 << 20,
            transcendentals=2 * CHIP * CHIP * HEADS,
        ),
        name="backward",
    )(scalars, after, after, after, own, own, before, before, att, log, up_own, up_oth, *ws)


def weight_kernel(s_ref, on_ref, up_t, att, keep, give):
    width = att.shape[2]
    rows = [[up_t[i, CHIP:, b * CHIP : (b + 1) * CHIP] for i in range(4)] for b in range(4)]
    left = jnp.concatenate([jnp.concatenate(row, axis=1) for row in rows], axis=0)
    total = dot(left, att[...].reshape(4 * CHIP, width), 1, 0)
    total = total.reshape(32, 2, 8, width)
    halves = [total[:, half].reshape(256, width) for half in range(2)]
    keep[...] = jnp.where(s_ref[3] == 0, halves[0], halves[1]).astype(BF)
    give[...] = jnp.where(s_ref[3] == 0, halves[1], halves[0]).astype(BF)


def weight_partial(scalars, got, sent):
    tile = 512
    return call(
        weight_kernel, "weight_partial", (HALF // tile,),
        [AFTER, whole(4, CHIP + TOK, HALF), pl.BlockSpec((4, CHIP, tile), lambda n, s: (0, 0, n))],
        [pl.BlockSpec((256, tile), lambda n, s: (0, n))] * 2, [bf(256, HALF)] * 2,
        2 * CHIP * D * HALF, 4 << 20,
    )(scalars, sent, got, got)


def plus(*terms):
    total = terms[0].astype(F32)
    for t in terms[1:]:
        total = total + t.astype(F32)
    return total


def merge_kernel(s_ref, own, back, mine, theirs):
    for i in range(2):
        total = plus(own[i], back[i]).astype(BF)
        mine[i], theirs[i] = total[:TOK], total[TOK:]


def merge(scalars, own, back):
    tile = 512
    part = lambda rows: pl.BlockSpec((2, rows, tile), lambda i, s: (0, 0, i))
    return call(
        merge_kernel, "merge", (HALF // tile,), [part(CHIP)] * 2, [part(TOK)] * 2, [bf(2, TOK, HALF)] * 2, 0, 3 << 20
    )(scalars, own, back)


def finish_kernel(s_ref, on_s, on_x, rest_s, rest_x, grad_q, grad_kv):
    for first, on, rest in ((s_ref[0], on_s, rest_s), (1 - s_ref[0], on_x, rest_x)):
        cols = pl.ds(pl.multiple_of(first * HALF, HALF), HALF)
        grad_q[:, cols] = on[0]
        for i in range(2):
            grad_kv[i, :, cols] = plus(on[1 + i], rest[i]).astype(BF)


def finish(scalars, *terms):
    return call(
        finish_kernel, "finish", (1,), [whole(n, TOK, HALF) for n in (3, 3, 2, 2)],
        [whole(TOK, D), whole(2, TOK, D)], [bf(TOK, D), bf(2, TOK, D)], 0, 5 << 20,
    )(scalars, *terms)


def pair_kernel(s_ref, grad_ref, keep, got, out):
    out[...] = plus(keep[...], got[...]).astype(BF)


def sum_up(scalars, keep, give, grad):
    tile = 512
    cols = pl.BlockSpec((256, tile), lambda n, s: (0, n))
    part = call(
        pair_kernel, "pair", (HALF // tile,), [AFTER, cols, cols], cols, bf(256, HALF), 0, 2 << 20
    )(scalars, grad, keep, to_y_neighbour(give))
    part = lax.all_to_all(part.reshape(32, 8, HALF), CTX, 0, 0, tiled=True)
    part = jnp.sum(part.reshape(16, 2, 8, HALF).astype(F32), axis=0)
    return jnp.concatenate([part[0], part[1]], axis=1)


def shards(queries, keys_values, upstream, out_weight):
    core = lax.axis_index("core")
    x, yh = lax.axis_index("x"), lax.axis_index("yh")
    chip = (lax.axis_index("yl") * 8 + lax.axis_index("z") + 1) & 15
    scalars = jnp.stack([core, chip, x, yh, lax.axis_index("yl")]).astype(jnp.int32)

    w = lax.dynamic_slice_in_dim(out_weight, core * HALF, HALF, 1)
    w_y, left, right = to_y_neighbour(w), to_x(w, 1), to_x(w, -1)
    up_own = to_chip(upstream[0], -1)
    left_y, right_y = meet(scalars, w_y, left, right)
    left_y, right_y = to_x(left_y, 1), to_x(right_y, -1)
    far_a, far_b = to_x(left_y[:128], 1), to_x(right_y[128:256], -1)
    kv = jnp.swapaxes(keys_values[0], 0, 1)
    mine, theirs = cut(scalars, queries[0], kv)
    up_oth = to_core(up_own)
    mine = pack(scalars, mine, to_core(theirs), up_oth)
    after, before = to_chip(mine, -1), to_chip(mine, 1)
    up_t = turn(scalars, up_own, up_oth)

    sent, log = forward(scalars, far_a, far_b, after, mine, before, up_t)
    got = lax.all_to_all(sent, "x", 0, 0, tiled=True)
    on_s, on_x, own, back = backward(
        scalars, after, mine, before, sent, log, up_own, up_oth, w, w_y, left, right, left_y, right_y, far_a, far_b
    )
    on_s, on_x = to_chip(on_s, 1), to_chip(on_x, 1, True)
    rest_s, rest_x = merge(scalars, own, to_chip(back, -1))
    rest_x = to_core(rest_x)
    keep, give = weight_partial(scalars, got, on_s)
    grad_q, grad_kv = finish(scalars, on_s, on_x, rest_s, rest_x)
    grad_weight = sum_up(scalars, keep, give, on_x)
    return grad_q[None], jnp.swapaxes(grad_kv, 0, 1)[None], grad_weight


def solution(mesh):
    names = tuple(name for name, _ in SPLIT)
    fine = Mesh(mesh.devices.reshape([size for _, size in SPLIT]), names)
    return jax.shard_map(
        shards,
        mesh=fine,
        in_specs=(P(FSDP, CTX, None), P(FSDP, CTX, None, None), P(FSDP, CTX, None), P(FSDP, None)),
        out_specs=(P(FSDP, CTX, None), P(FSDP, CTX, None, None), P(CTX + FSDP, None)),
        check_vma=False,
    )
```

```python
import jax
import jax.numpy as jnp
from jax import lax
from jax.experimental import pallas as pl
from jax.experimental.pallas import tpu as pltpu
from jax.sharding import Mesh
from jax.sharding import PartitionSpec as P

SPLIT = (("yl", 2), ("z", 8), ("core", 2), ("x", 4), ("yh", 2))
CTX = ("yl", "z", "core")
FSDP = ("x", "yh")

TOK = 128
CHIP = 256
HEADS = 8
HD = 128
HALF = HEADS * HD
D = 2048
TOGETHER = 2
STEPS = HEADS // TOGETHER
WIDE = TOGETHER * HD
NEGATIVE = -1e30
INV_ROOT = HD**-0.5
BF = jnp.bfloat16
F32 = jnp.float32
VMEM = {"cut": 56, "forward": 56, "backward": 56, "weight_partial": 56, "finish": 56, "merge": 16, "pair": 8, "meet": 8, "pack": 8, "turn": 8, "add_y": 8}


def dot(a, b, ca, cb):
    return lax.dot_general(a, b, (((ca,), (cb,)), ((), ())), preferred_element_type=F32)


def to_chip(a, by, cross=False):
    pairs = []
    for i in range(16):
        for core in range(2):
            pairs.append((2 * i + core, (i + by) % 16 * 2 + (1 - core if cross else core)))
    return lax.ppermute(a, CTX, pairs)


def to_core(a):
    return lax.ppermute(a, "core", [(0, 1), (1, 0)])


def to_x(a, by):
    return lax.ppermute(a, "x", [(i, (i + by) % 4) for i in range(4)])


def to_y_neighbour(a):
    return lax.ppermute(a, ("yl", "yh"), [(0, 3), (3, 0), (1, 2), (2, 1)])


def call(body, name, grid, in_specs, out_specs, out_shape, flops, moved, exps=0):
    return pl.pallas_call(
        body,
        grid_spec=pltpu.PrefetchScalarGridSpec(
            num_scalar_prefetch=1, grid=grid, in_specs=in_specs, out_specs=out_specs
        ),
        out_shape=out_shape,
        compiler_params=pltpu.CompilerParams(vmem_limit_bytes=VMEM[name] << 20),
        cost_estimate=pl.CostEstimate(flops=flops, bytes_accessed=moved, transcendentals=exps),
        name=name,
    )


AFTER = pl.BlockSpec(memory_space=pl.ANY)


def whole(*shape):
    return pl.BlockSpec(shape, lambda *_: (0,) * len(shape))


def bf(*shape):
    return jax.ShapeDtypeStruct(shape, BF)


def cut_kernel(s_ref, q, kv, mine, theirs):
    own = s_ref[0] * HALF
    for first, out in ((own, mine), (HALF - own, theirs)):
        at = pl.ds(pl.multiple_of(first, HALF), HALF)
        out[:, :HALF] = q[:, at]
        out[:, HALF : 2 * HALF] = kv[0, :, at]
        out[:, 2 * HALF :] = kv[1, :, at]


def cut(scalars, q, kv):
    return call(
        cut_kernel, "cut", (1,), [whole(TOK, D), whole(2, TOK, D)], [whole(TOK, 3 * HALF)] * 2,
        [bf(TOK, 3 * HALF)] * 2, 0, 4 << 20,
    )(scalars, q, kv)


def pack_kernel(s_ref, *refs):
    mine, got, out = refs[-3:]
    rows = mine.shape[0]
    out[:rows] = mine[...]
    out[rows:] = got[...]


def pack(scalars, mine, got, *first):
    rows, width = mine.shape
    part = lambda n: pl.BlockSpec((n, HALF), lambda i, s: (0, i))
    return call(
        pack_kernel, "pack", (width // HALF,), [AFTER] * len(first) + [part(rows)] * 2, part(2 * rows),
        bf(2 * rows, width), 0, 8 * rows * width,
    )(scalars, *first, mine, got)


def meet_kernel(s_ref, w_y, from_left, from_right, to_right, to_left):
    to_right[:256], to_right[256:] = w_y[...], from_left[:128]
    to_left[:256], to_left[256:] = w_y[...], from_right[128:]


def meet(scalars, w_y, from_left, from_right):
    return call(
        meet_kernel, "meet", (1,), [whole(256, HALF)] * 3, [whole(384, HALF)] * 2, [bf(384, HALF)] * 2, 0, 3 << 20
    )(scalars, w_y, from_left, from_right)


def turn_kernel(s_ref, up_own, up_oth, out):
    for i, up in enumerate((up_own, up_oth)):
        turned = up[...].T.reshape(8, 4, 16, TOK)
        for to in range(4):
            out[to, :, i * TOK : (i + 1) * TOK] = turned[:, to].reshape(TOK, TOK)


def turn(scalars, up_own, up_oth):
    quarter = pl.BlockSpec((TOK, 512), lambda b, s: (0, b))
    return call(
        turn_kernel, "turn", (4,), [quarter] * 2, pl.BlockSpec((4, TOK, CHIP), lambda b, s: (0, 0, b)),
        bf(4, TOK, HALF), 0, 2 << 20,
    )(scalars, up_own, up_oth)


PIECES = (
    (0, 0, 0, 256), (0, 1, 0, 256), (3, 0, 0, 256), (1, 0, 0, 256), (3, 1, 0, 256), (2, 0, 0, 128),
    (1, 1, 0, 256), (2, 0, 128, 128), (2, 1, 0, 128), (2, 1, 128, 128),
)


def scores(s_ref, q, k0, k1, k2):
    core, chip = s_ref[0], s_ref[1]
    key_at = (lax.broadcasted_iota(jnp.int32, (CHIP, CHIP), 0) + core * TOK) & (CHIP - 1)
    query_at = (lax.broadcasted_iota(jnp.int32, (CHIP, CHIP), 1) + core * TOK) & (CHIP - 1)
    near = key_at <= query_at
    shown = jnp.logical_or(near, chip >= 2)
    sm = jnp.where(near, dot(k0, q, 1, 1), dot(k2, q, 1, 1)) * INV_ROOT
    sm = jnp.where(shown, sm, NEGATIVE)
    s1 = jnp.where(chip >= 1, dot(k1, q, 1, 1) * INV_ROOT, NEGATIVE)
    return near, sm, s1


def split(near, pm):
    return jnp.where(near, pm, 0.0).astype(BF), jnp.where(near, 0.0, pm).astype(BF)


def forward_kernel(s_ref, wa_ref, wb_ref, q_r, k0_r, v0_r, k1_r, v1_r, k2_r, v2_r, up_t, out_r, log_r):
    out_r[:, CHIP:] = up_t[...]
    for i in range(TOGETHER):
        h = slice(i * HD, (i + 1) * HD)
        near, sm, s1 = scores(s_ref, q_r[:, h], k0_r[:, h], k1_r[:, h], k2_r[:, h])
        top = jnp.maximum(jnp.max(sm, axis=0, keepdims=True), jnp.max(s1, axis=0, keepdims=True))
        em = jnp.exp(sm - top)
        e1 = jnp.exp(s1 - top)
        total = jnp.sum(em, axis=0, keepdims=True) + jnp.sum(e1, axis=0, keepdims=True)
        log_r[i] = top + jnp.log(total)
        scale = 1.0 / total
        p0, p2 = split(near, em * scale)
        p1 = (e1 * scale).astype(BF)
        att = dot(v0_r[:, h].T, p0, 1, 0) + dot(v1_r[:, h].T, p1, 1, 0) + dot(v2_r[:, h].T, p2, 1, 0)
        att = att.astype(BF).T
        for to in range(4):
            out_r[to, :CHIP, h] = att


def at(first):
    return pl.BlockSpec((CHIP, WIDE), lambda h, s: (0, first * STEPS + h))


def deep(n, rows):
    return pl.BlockSpec((n, rows, WIDE), lambda h, s: (0, 0, h))


LOGS = pl.BlockSpec((TOGETHER, 1, CHIP), lambda h, s: (h, 0, 0))


def forward(scalars, wa, wb, after, own, before, up_t):
    return call(
        forward_kernel, "forward", (STEPS,), [AFTER, AFTER, at(0), at(1), at(2), at(1), at(2), at(1), at(2), deep(4, TOK)],
        [deep(4, CHIP + TOK), LOGS], [bf(4, CHIP + TOK, HALF), jax.ShapeDtypeStruct((HEADS, 1, CHIP), F32)],
        2 * 6 * CHIP * CHIP * HD * HEADS, 6 << 20, 2 * CHIP * CHIP * HEADS,
    )(scalars, wa, wb, after, after, after, own, own, before, before, up_t)


def backward_kernel(
    s_ref, q_r, k0_r, v0_r, k1_r, v1_r, k2_r, v2_r, att_r, log_r, up_own, up_oth, *rest
):
    ws, (on_r, own_r, back_r, up) = rest[:8], rest[8:]
    x, yh = s_ref[2], s_ref[3]

    @pl.when(pl.program_id(0) == 0)
    def _():
        start = 0
        for dx, dy, first, size in PIECES:
            block = ((x + dx) & 3) * 2 + ((yh + dy) & 1)
            cols = pl.ds(pl.multiple_of(block * 256 + first, 128), size)
            up[:TOK, start : start + size] = up_own[:, cols]
            up[TOK:, start : start + size] = up_oth[:, cols]
            start += size

    w = jnp.concatenate([r[...] for r in ws], axis=0)
    grads = dot(up[...], w, 1, 0).astype(BF)
    for i in range(TOGETHER):
        h = slice(i * HD, (i + 1) * HD)
        q, do = q_r[:, h], grads[:, h]
        k0, k1, k2 = k0_r[:, h], k1_r[:, h], k2_r[:, h]
        near, sm, s1 = scores(s_ref, q, k0, k1, k2)
        pm = jnp.exp(sm - log_r[i])
        p1 = jnp.exp(s1 - log_r[i])
        p0_low, p2_low = split(near, pm)
        p1_low = p1.astype(BF)
        center = jnp.sum((do.astype(F32) * att_r[0, :, h].astype(F32)).T, axis=0, keepdims=True)
        dm = pm * (jnp.where(near, dot(v0_r[:, h], do, 1, 1), dot(v2_r[:, h], do, 1, 1)) - center)
        d1 = (p1 * (dot(v1_r[:, h], do, 1, 1) - center)).astype(BF)
        d0, d2 = split(near, dm)
        dq = dot(k0.T, d0, 1, 0) + dot(k1.T, d1, 1, 0) + dot(k2.T, d2, 1, 0)
        dq = (dq * INV_ROOT).astype(BF).T
        on_r[0, :, h] = dq
        for out, n, d, p in ((on_r, 1, d0, p0_low), (own_r, 0, d1, p1_low), (back_r, 0, d2, p2_low)):
            out[n, :, h] = (dot(d, q, 1, 0) * INV_ROOT).astype(BF)
            out[n + 1, :, h] = dot(p, do, 1, 0).astype(BF)


def backward(scalars, after, own, before, att, log, up_own, up_oth, *ws):
    cols = lambda rows: pl.BlockSpec((rows, WIDE), lambda h, s: (0, h))
    return pl.pallas_call(
        backward_kernel,
        grid_spec=pltpu.PrefetchScalarGridSpec(
            num_scalar_prefetch=1,
            grid=(STEPS,),
            in_specs=[at(0), at(1), at(2), at(1), at(2), at(1), at(2), deep(1, CHIP), LOGS, whole(TOK, D), whole(TOK, D)]
            + [cols(rows) for rows in (256, 256, 256, 256, 384, 384, 128, 128)],
            out_specs=[deep(n, CHIP) for n in (3, 2, 2)],
            scratch_shapes=[pltpu.VMEM((CHIP, D), BF)],
        ),
        out_shape=[bf(n, CHIP, HALF) for n in (3, 2, 2)],
        compiler_params=pltpu.CompilerParams(vmem_limit_bytes=VMEM["backward"] << 20),
        cost_estimate=pl.CostEstimate(
            flops=2 * CHIP * (15 * CHIP * HD * HEADS + D * HALF), bytes_accessed=18 << 20,
            transcendentals=2 * CHIP * CHIP * HEADS,
        ),
        name="backward",
    )(scalars, after, after, after, own, own, before, before, att, log, up_own, up_oth, *ws)


def weight_kernel(s_ref, back_ref, up_t, att, out):
    rows = [[up_t[i, CHIP:, b * CHIP : (b + 1) * CHIP] for i in range(4)] for b in range(4)]
    left = jnp.concatenate([jnp.concatenate(row, axis=1) for row in rows], axis=0)
    out[...] = dot(left, att[...].reshape(4 * CHIP, att.shape[2]), 1, 0).astype(BF)


def weight_partial(scalars, got, sent):
    tile = 512
    return call(
        weight_kernel, "weight_partial", (HALF // tile,),
        [AFTER, whole(4, CHIP + TOK, HALF), pl.BlockSpec((4, CHIP, tile), lambda n, s: (0, 0, n))],
        pl.BlockSpec((512, tile), lambda n, s: (0, n)), bf(512, HALF), 2 * CHIP * D * HALF, 4 << 20,
    )(scalars, sent, got, got)


def plus(*terms):
    total = terms[0].astype(F32)
    for t in terms[1:]:
        total = total + t.astype(F32)
    return total


def merge_kernel(s_ref, on, own, back, mine, theirs):
    for out, rows in ((mine, slice(0, TOK)), (theirs, slice(TOK, CHIP))):
        out[0] = on[0, rows]
        for i in range(2):
            out[1 + i] = plus(on[1 + i, rows], own[i, rows], back[i, rows]).astype(BF)


def merge(scalars, on, own, back):
    tile = 512
    part = lambda n, rows: pl.BlockSpec((n, rows, tile), lambda i, s: (0, 0, i))
    return call(
        merge_kernel, "merge", (HALF // tile,), [part(3, CHIP), part(2, CHIP), part(2, CHIP)], [part(3, TOK)] * 2,
        [bf(3, TOK, HALF)] * 2, 0, 5 << 20,
    )(scalars, on, own, back)


def finish_kernel(s_ref, mine, theirs, grad_q, grad_kv):
    for first, part in ((s_ref[0], mine), (1 - s_ref[0], theirs)):
        cols = pl.ds(pl.multiple_of(first * HALF, HALF), HALF)
        grad_q[:, cols] = part[0]
        for i in range(2):
            grad_kv[i, :, cols] = part[1 + i]


def finish(scalars, mine, theirs):
    return call(
        finish_kernel, "finish", (1,), [whole(3, TOK, HALF)] * 2, [whole(TOK, D), whole(2, TOK, D)],
        [bf(TOK, D), bf(2, TOK, D)], 0, 3 << 20,
    )(scalars, mine, theirs)


def sum_up(part):
    part = lax.all_to_all(part.reshape(64, 8, HALF), CTX + ("yh",), 0, 0, tiled=True)
    part = jnp.sum(part.reshape(16, 2, 2, 8, HALF).astype(F32), axis=(0, 2))
    return jnp.concatenate([part[0], part[1]], axis=1)


def shards(queries, keys_values, upstream, out_weight):
    core = lax.axis_index("core")
    x, yh = lax.axis_index("x"), lax.axis_index("yh")
    chip = (lax.axis_index("yl") * 8 + lax.axis_index("z") + 1) & 15
    scalars = jnp.stack([core, chip, x, yh, lax.axis_index("yl")]).astype(jnp.int32)

    w = lax.dynamic_slice_in_dim(out_weight, core * HALF, HALF, 1)
    w_y, left, right = to_y_neighbour(w), to_x(w, 1), to_x(w, -1)
    up_own = to_chip(upstream[0], -1)
    left_y, right_y = meet(scalars, w_y, left, right)
    left_y, right_y = to_x(left_y, 1), to_x(right_y, -1)
    far_a, far_b = to_x(left_y[:128], 1), to_x(right_y[128:256], -1)
    kv = jnp.swapaxes(keys_values[0], 0, 1)
    mine, theirs = cut(scalars, queries[0], kv)
    up_oth = to_core(up_own)
    mine = pack(scalars, mine, to_core(theirs), up_oth)
    after, before = to_chip(mine, -1), to_chip(mine, 1)
    up_t = turn(scalars, up_own, up_oth)

    sent, log = forward(scalars, far_a, far_b, after, mine, before, up_t)
    got = lax.all_to_all(sent, "x", 0, 0, tiled=True)
    on, own, back = backward(
        scalars, after, mine, before, sent, log, up_own, up_oth, w, w_y, left, right, left_y, right_y, far_a, far_b
    )
    on, back = to_chip(on, 1), to_chip(back, -1)
    part = weight_partial(scalars, got, back)
    mine, theirs = merge(scalars, on, own, back)
    grad_q, grad_kv = finish(scalars, mine, to_core(theirs))
    grad_weight = sum_up(part)
    return grad_q[None], jnp.swapaxes(grad_kv, 0, 1)[None], grad_weight


def solution(mesh):
    names = tuple(name for name, _ in SPLIT)
    fine = Mesh(mesh.devices.reshape([size for _, size in SPLIT]), names)
    return jax.shard_map(
        shards,
        mesh=fine,
        in_specs=(P(FSDP, CTX, None), P(FSDP, CTX, None, None), P(FSDP, CTX, None), P(FSDP, None)),
        out_specs=(P(FSDP, CTX, None), P(FSDP, CTX, None, None), P(CTX + FSDP, None)),
        check_vma=False,
    )
```

```python
import jax
import jax.numpy as jnp
from jax import lax
from jax.experimental import pallas as pl
from jax.experimental.pallas import tpu as pltpu
from jax.sharding import Mesh
from jax.sharding import PartitionSpec as P

SPLIT = (("yl", 2), ("z", 8), ("core", 2), ("x", 4), ("yh", 2))
CTX = ("yl", "z", "core")
FSDP = ("x", "yh")

TOK = 128
CHIP = 256
HEADS = 8
HD = 128
HALF = HEADS * HD
D = 2048
TOGETHER = 2
STEPS = HEADS // TOGETHER
WIDE = TOGETHER * HD
NEGATIVE = -1e30
INV_ROOT = HD**-0.5
BF = jnp.bfloat16
F32 = jnp.float32
VMEM = {"cut": 56, "forward": 56, "backward": 56, "weight_partial": 56, "finish": 56, "merge": 16, "pair": 8, "meet": 8, "pack": 8, "turn": 8, "add_y": 8}


def dot(a, b, ca, cb):
    return lax.dot_general(a, b, (((ca,), (cb,)), ((), ())), preferred_element_type=F32)


def to_chip(a, by, cross=False):
    pairs = []
    for i in range(16):
        for core in range(2):
            pairs.append((2 * i + core, (i + by) % 16 * 2 + (1 - core if cross else core)))
    return lax.ppermute(a, CTX, pairs)


def to_core(a):
    return lax.ppermute(a, "core", [(0, 1), (1, 0)])


def to_x(a, by):
    return lax.ppermute(a, "x", [(i, (i + by) % 4) for i in range(4)])


def to_y_neighbour(a):
    return lax.ppermute(a, ("yl", "yh"), [(0, 3), (3, 0), (1, 2), (2, 1)])


def call(body, name, grid, in_specs, out_specs, out_shape, flops, moved, exps=0):
    return pl.pallas_call(
        body,
        grid_spec=pltpu.PrefetchScalarGridSpec(
            num_scalar_prefetch=1, grid=grid, in_specs=in_specs, out_specs=out_specs
        ),
        out_shape=out_shape,
        compiler_params=pltpu.CompilerParams(vmem_limit_bytes=VMEM[name] << 20),
        cost_estimate=pl.CostEstimate(flops=flops, bytes_accessed=moved, transcendentals=exps),
        name=name,
    )


AFTER = pl.BlockSpec(memory_space=pl.ANY)


def whole(*shape):
    return pl.BlockSpec(shape, lambda *_: (0,) * len(shape))


def bf(*shape):
    return jax.ShapeDtypeStruct(shape, BF)


def cut_kernel(s_ref, q, kv, mine, theirs):
    own = s_ref[0] * HALF
    for first, out in ((own, mine), (HALF - own, theirs)):
        at = pl.ds(pl.multiple_of(first, HALF), HALF)
        out[:, :HALF] = q[:, at]
        out[:, HALF : 2 * HALF] = kv[0, :, at]
        out[:, 2 * HALF :] = kv[1, :, at]


def cut(scalars, q, kv):
    return call(
        cut_kernel, "cut", (1,), [whole(TOK, D), whole(2, TOK, D)], [whole(TOK, 3 * HALF)] * 2,
        [bf(TOK, 3 * HALF)] * 2, 0, 4 << 20,
    )(scalars, q, kv)


def pack_kernel(s_ref, *refs):
    mine, got, out = refs[-3:]
    rows = mine.shape[0]
    out[:rows] = mine[...]
    out[rows:] = got[...]


def pack(scalars, mine, got, *first):
    rows, width = mine.shape
    part = lambda n: pl.BlockSpec((n, HALF), lambda i, s: (0, i))
    return call(
        pack_kernel, "pack", (width // HALF,), [AFTER] * len(first) + [part(rows)] * 2, part(2 * rows),
        bf(2 * rows, width), 0, 8 * rows * width,
    )(scalars, *first, mine, got)


def meet_kernel(s_ref, w_y, from_left, from_right, up, to_right, to_left, up_out):
    up_out[...] = up[...]
    to_right[:256], to_right[256:] = w_y[...], from_left[:128]
    to_left[:256], to_left[256:] = w_y[...], from_right[128:]


def meet(scalars, w_y, from_left, from_right, up):
    return call(
        meet_kernel, "meet", (1,), [whole(256, HALF)] * 3 + [whole(TOK, D)], [whole(384, HALF)] * 2 + [whole(TOK, D)],
        [bf(384, HALF)] * 2 + [bf(TOK, D)], 0, 4 << 20,
    )(scalars, w_y, from_left, from_right, up)


def turn_kernel(s_ref, wa_ref, wb_ref, up_own, up_oth, out):
    for i, up in enumerate((up_own, up_oth)):
        turned = up[...].T.reshape(8, 4, 16, TOK)
        for to in range(4):
            out[to, :, i * TOK : (i + 1) * TOK] = turned[:, to].reshape(TOK, TOK)


def turn(scalars, wa, wb, up_own, up_oth):
    quarter = pl.BlockSpec((TOK, 512), lambda b, s: (0, b))
    return call(
        turn_kernel, "turn", (4,), [AFTER] * 2 + [quarter] * 2, pl.BlockSpec((4, TOK, CHIP), lambda b, s: (0, 0, b)),
        bf(4, TOK, HALF), 0, 2 << 20,
    )(scalars, wa, wb, up_own, up_oth)


PIECES = (
    (0, 0, 0, 256), (0, 1, 0, 256), (3, 0, 0, 256), (1, 0, 0, 256), (3, 1, 0, 256), (2, 0, 0, 128),
    (1, 1, 0, 256), (2, 0, 128, 128), (2, 1, 0, 128), (2, 1, 128, 128),
)


def scores(s_ref, q, k0, k1, k2):
    core, chip = s_ref[0], s_ref[1]
    key_at = (lax.broadcasted_iota(jnp.int32, (CHIP, CHIP), 0) + core * TOK) & (CHIP - 1)
    query_at = (lax.broadcasted_iota(jnp.int32, (CHIP, CHIP), 1) + core * TOK) & (CHIP - 1)
    near = key_at <= query_at
    shown = jnp.logical_or(near, chip >= 2)
    sm = jnp.where(near, dot(k0, q, 1, 1), dot(k2, q, 1, 1)) * INV_ROOT
    sm = jnp.where(shown, sm, NEGATIVE)
    s1 = jnp.where(chip >= 1, dot(k1, q, 1, 1) * INV_ROOT, NEGATIVE)
    return near, sm, s1


def split(near, pm):
    return jnp.where(near, pm, 0.0).astype(BF), jnp.where(near, 0.0, pm).astype(BF)


def forward_kernel(s_ref, turned_ref, q_r, k0_r, v0_r, k1_r, v1_r, k2_r, v2_r, out_r, log_r):
    for i in range(TOGETHER):
        h = slice(i * HD, (i + 1) * HD)
        near, sm, s1 = scores(s_ref, q_r[:, h], k0_r[:, h], k1_r[:, h], k2_r[:, h])
        top = jnp.maximum(jnp.max(sm, axis=0, keepdims=True), jnp.max(s1, axis=0, keepdims=True))
        em = jnp.exp(sm - top)
        e1 = jnp.exp(s1 - top)
        total = jnp.sum(em, axis=0, keepdims=True) + jnp.sum(e1, axis=0, keepdims=True)
        log_r[i] = top + jnp.log(total)
        scale = 1.0 / total
        p0, p2 = split(near, em * scale)
        p1 = (e1 * scale).astype(BF)
        att = dot(v0_r[:, h].T, p0, 1, 0) + dot(v1_r[:, h].T, p1, 1, 0) + dot(v2_r[:, h].T, p2, 1, 0)
        att = att.astype(BF).T
        for to in range(4):
            out_r[to, :, h] = att


def at(first):
    return pl.BlockSpec((CHIP, WIDE), lambda h, s: (0, first * STEPS + h))


def deep(n, rows):
    return pl.BlockSpec((n, rows, WIDE), lambda h, s: (0, 0, h))


LOGS = pl.BlockSpec((TOGETHER, 1, CHIP), lambda h, s: (h, 0, 0))


def forward(scalars, turned, after, own, before):
    return call(
        forward_kernel, "forward", (STEPS,), [AFTER, at(0), at(1), at(2), at(1), at(2), at(1), at(2)],
        [deep(4, CHIP), LOGS], [bf(4, CHIP, HALF), jax.ShapeDtypeStruct((HEADS, 1, CHIP), F32)],
        2 * 6 * CHIP * CHIP * HD * HEADS, 6 << 20, 2 * CHIP * CHIP * HEADS,
    )(scalars, turned, after, after, after, own, own, before, before)


def backward_kernel(
    s_ref, q_r, k0_r, v0_r, k1_r, v1_r, k2_r, v2_r, att_r, log_r, up_own, up_oth, *rest
):
    ws, (on_r, own_r, back_r, up) = rest[:8], rest[8:]
    x, yh = s_ref[2], s_ref[3]

    @pl.when(pl.program_id(0) == 0)
    def _():
        start = 0
        for dx, dy, first, size in PIECES:
            block = ((x + dx) & 3) * 2 + ((yh + dy) & 1)
            cols = pl.ds(pl.multiple_of(block * 256 + first, 128), size)
            up[:TOK, start : start + size] = up_own[:, cols]
            up[TOK:, start : start + size] = up_oth[:, cols]
            start += size

    w = jnp.concatenate([r[...] for r in ws], axis=0)
    grads = dot(up[...], w, 1, 0).astype(BF)
    for i in range(TOGETHER):
        h = slice(i * HD, (i + 1) * HD)
        q, do = q_r[:, h], grads[:, h]
        k0, k1, k2 = k0_r[:, h], k1_r[:, h], k2_r[:, h]
        near, sm, s1 = scores(s_ref, q, k0, k1, k2)
        pm = jnp.exp(sm - log_r[i])
        p1 = jnp.exp(s1 - log_r[i])
        p0_low, p2_low = split(near, pm)
        p1_low = p1.astype(BF)
        center = jnp.sum((do.astype(F32) * att_r[0, :, h].astype(F32)).T, axis=0, keepdims=True)
        dm = pm * (jnp.where(near, dot(v0_r[:, h], do, 1, 1), dot(v2_r[:, h], do, 1, 1)) - center)
        d1 = (p1 * (dot(v1_r[:, h], do, 1, 1) - center)).astype(BF)
        d0, d2 = split(near, dm)
        dq = dot(k0.T, d0, 1, 0) + dot(k1.T, d1, 1, 0) + dot(k2.T, d2, 1, 0)
        dq = (dq * INV_ROOT).astype(BF).T
        on_r[0, :, h] = dq
        for out, n, d, p in ((on_r, 1, d0, p0_low), (own_r, 0, d1, p1_low), (back_r, 0, d2, p2_low)):
            out[n, :, h] = (dot(d, q, 1, 0) * INV_ROOT).astype(BF)
            out[n + 1, :, h] = dot(p, do, 1, 0).astype(BF)


def backward(scalars, after, own, before, att, log, up_own, up_oth, *ws):
    cols = lambda rows: pl.BlockSpec((rows, WIDE), lambda h, s: (0, h))
    return pl.pallas_call(
        backward_kernel,
        grid_spec=pltpu.PrefetchScalarGridSpec(
            num_scalar_prefetch=1,
            grid=(STEPS,),
            in_specs=[at(0), at(1), at(2), at(1), at(2), at(1), at(2), deep(1, CHIP), LOGS, whole(TOK, D), whole(TOK, D)]
            + [cols(rows) for rows in (256, 256, 256, 256, 384, 384, 128, 128)],
            out_specs=[deep(n, CHIP) for n in (3, 2, 2)],
            scratch_shapes=[pltpu.VMEM((CHIP, D), BF)],
        ),
        out_shape=[bf(n, CHIP, HALF) for n in (3, 2, 2)],
        compiler_params=pltpu.CompilerParams(vmem_limit_bytes=VMEM["backward"] << 20),
        cost_estimate=pl.CostEstimate(
            flops=2 * CHIP * (15 * CHIP * HD * HEADS + D * HALF), bytes_accessed=18 << 20,
            transcendentals=2 * CHIP * CHIP * HEADS,
        ),
        name="backward",
    )(scalars, after, after, after, own, own, before, before, att, log, up_own, up_oth, *ws)


def weight_kernel(s_ref, up_t, att, keep, give):
    width = att.shape[2]
    rows = [[up_t[i, :, b * CHIP : (b + 1) * CHIP] for i in range(4)] for b in range(4)]
    left = jnp.concatenate([jnp.concatenate(row, axis=1) for row in rows], axis=0)
    total = dot(left, att[...].reshape(4 * CHIP, width), 1, 0)
    total = total.reshape(32, 2, 8, width)
    halves = [total[:, half].reshape(256, width) for half in range(2)]
    keep[...] = jnp.where(s_ref[3] == 0, halves[0], halves[1]).astype(BF)
    give[...] = jnp.where(s_ref[3] == 0, halves[1], halves[0]).astype(BF)


def weight_partial(scalars, up_t, att):
    tile = 512
    return call(
        weight_kernel, "weight_partial", (HALF // tile,),
        [whole(4, TOK, HALF), pl.BlockSpec((4, CHIP, tile), lambda n, s: (0, 0, n))],
        [pl.BlockSpec((256, tile), lambda n, s: (0, n))] * 2, [bf(256, HALF)] * 2,
        2 * CHIP * D * HALF, 4 << 20,
    )(scalars, up_t, att)


def plus(*terms):
    total = terms[0].astype(F32)
    for t in terms[1:]:
        total = total + t.astype(F32)
    return total


def merge_kernel(s_ref, on, own, back, mine, theirs):
    for out, rows in ((mine, slice(0, TOK)), (theirs, slice(TOK, CHIP))):
        out[0] = on[0, rows]
        for i in range(2):
            out[1 + i] = plus(on[1 + i, rows], own[i, rows], back[i, rows]).astype(BF)


def merge(scalars, on, own, back):
    tile = 512
    part = lambda n, rows: pl.BlockSpec((n, rows, tile), lambda i, s: (0, 0, i))
    return call(
        merge_kernel, "merge", (HALF // tile,), [part(3, CHIP), part(2, CHIP), part(2, CHIP)], [part(3, TOK)] * 2,
        [bf(3, TOK, HALF)] * 2, 0, 5 << 20,
    )(scalars, on, own, back)


def finish_kernel(s_ref, mine, theirs, grad_q, grad_kv):
    for first, part in ((s_ref[0], mine), (1 - s_ref[0], theirs)):
        cols = pl.ds(pl.multiple_of(first * HALF, HALF), HALF)
        grad_q[:, cols] = part[0]
        for i in range(2):
            grad_kv[i, :, cols] = part[1 + i]


def finish(scalars, mine, theirs):
    return call(
        finish_kernel, "finish", (1,), [whole(3, TOK, HALF)] * 2, [whole(TOK, D), whole(2, TOK, D)],
        [bf(TOK, D), bf(2, TOK, D)], 0, 3 << 20,
    )(scalars, mine, theirs)


def pair_kernel(s_ref, back_ref, keep, got, out):
    out[...] = plus(keep[...], got[...]).astype(BF)


def sum_up(scalars, keep, give, back):
    tile = 512
    cols = pl.BlockSpec((256, tile), lambda n, s: (0, n))
    part = call(pair_kernel, "pair", (HALF // tile,), [AFTER, cols, cols], cols, bf(256, HALF), 0, 2 << 20)(
        scalars, back, keep, to_y_neighbour(give)
    )
    part = lax.all_to_all(part.reshape(32, 8, HALF), CTX, 0, 0, tiled=True)
    part = jnp.sum(part.reshape(16, 2, 8, HALF).astype(F32), axis=0)
    return jnp.concatenate([part[0], part[1]], axis=1)


def shards(queries, keys_values, upstream, out_weight):
    core = lax.axis_index("core")
    x, yh = lax.axis_index("x"), lax.axis_index("yh")
    chip = (lax.axis_index("yl") * 8 + lax.axis_index("z") + 1) & 15
    scalars = jnp.stack([core, chip, x, yh, lax.axis_index("yl")]).astype(jnp.int32)

    w = lax.dynamic_slice_in_dim(out_weight, core * HALF, HALF, 1)
    w_y, left, right = to_y_neighbour(w), to_x(w, 1), to_x(w, -1)
    left_y, right_y, up_own = meet(scalars, w_y, left, right, to_chip(upstream[0], -1))
    left_y, right_y = to_x(left_y, 1), to_x(right_y, -1)
    far_a, far_b = to_x(left_y[:128], 1), to_x(right_y[128:256], -1)
    kv = jnp.swapaxes(keys_values[0], 0, 1)
    mine, theirs = cut(scalars, queries[0], kv)
    up_oth = to_core(up_own)
    mine = pack(scalars, mine, to_core(theirs), up_oth)
    after, before = to_chip(mine, -1), to_chip(mine, 1)
    turned = turn(scalars, far_a, far_b, up_own, up_oth)
    up_t = lax.all_to_all(turned, "x", 0, 0, tiled=True)

    sent, log = forward(scalars, turned, after, mine, before)
    got = lax.all_to_all(sent, "x", 0, 0, tiled=True)
    on, own, back = backward(
        scalars, after, mine, before, sent, log, up_own, up_oth, w, w_y, left, right, left_y, right_y, far_a, far_b
    )
    on, back = to_chip(on, 1), to_chip(back, -1)
    keep, give = weight_partial(scalars, up_t, got)
    mine, theirs = merge(scalars, on, own, back)
    grad_q, grad_kv = finish(scalars, mine, to_core(theirs))
    grad_weight = sum_up(scalars, keep, give, back)
    return grad_q[None], jnp.swapaxes(grad_kv, 0, 1)[None], grad_weight


def solution(mesh):
    names = tuple(name for name, _ in SPLIT)
    fine = Mesh(mesh.devices.reshape([size for _, size in SPLIT]), names)
    return jax.shard_map(
        shards,
        mesh=fine,
        in_specs=(P(FSDP, CTX, None), P(FSDP, CTX, None, None), P(FSDP, CTX, None), P(FSDP, None)),
        out_specs=(P(FSDP, CTX, None), P(FSDP, CTX, None, None), P(CTX + FSDP, None)),
        check_vma=False,
    )
```
